32 devices in a mesh: groups: 2 (over y), rows: 16 (over z, x, core), heads: 1.
Axes of the slice: x: 2, y: 2, z: 4, core: 2. Of those that a mesh axis runs over, the one named last changes fastest.
Arguments:
- query_in: bfloat16 [640, 1024], P(('groups', 'rows'), 'heads'), parts along dimension 0, may hold values from -6 to 6
- key_in: bfloat16 [640, 1024], P(('groups', 'rows'), 'heads'), parts along dimension 0, may hold values from -6 to 6
- value_in: bfloat16 [640, 2048], P(('groups', 'rows'), 'heads'), parts along dimension 0, may hold values from -6 to 6
- gate_in: bfloat16 [640, 2048], P(('groups', 'rows'), 'heads'), parts along dimension 0, may hold values from -6 to 6
- decay_in: float32 [640, 16], P(('groups', 'rows'), 'heads'), parts along dimension 0, may hold values from -6 to 6
- beta_in: float32 [640, 16], P(('groups', 'rows'), 'heads'), parts along dimension 0, may hold values from -6 to 6
- decay_rate: float32 [16], P('heads'), may hold values from 0.02 to 4
- decay_bias: float32 [16], P('heads'), may hold values from -1 to 1
- norm_gain: float32 [128], replicated, may hold values from 0.5 to 1.5
- prior_state: bfloat16 [160, 16, 128, 128], P(('groups', 'rows'), 'heads'), parts along dimension 0, may hold values from -4 to 4
- accepted: int32 [160], P(('groups', 'rows')), parts along dimension 0, may hold values from 1 to 4
- out_weight: bfloat16 [2048, 2048], P('heads', 'rows'), may hold values from -0.125 to 0.125
- residual: bfloat16 [640, 2048], P(('groups', 'rows'), 'heads'), parts along dimension 0, may hold values from -12 to 12
- post_gain: float32 [2048], P('heads'), may hold values from 0.5 to 1.5
- expert_ids: int32 [640, 10], P(('groups', 'rows')), parts along dimension 0, may hold values from 0 to 31, all different within a row; in each aligned block of 20 rows (0 to 19, 20 to 39, ...) at most 8 rows name the same one
- expert_scores: float32 [640, 10], P(('groups', 'rows')), parts along dimension 0, may hold values from 0.1 to 1
- expert_up: bfloat16 [32, 2048, 512], P('rows', 'heads'), may hold values from -0.125 to 0.125
- expert_down: bfloat16 [32, 256, 2048], P('rows', None, 'heads'), may hold values from -0.375 to 0.375
Outputs:
- layer_out: bfloat16 [640, 2048], P(('groups', 'rows'), 'heads'), parts along dimension 0
- kept_state: bfloat16 [160, 16, 128, 128], P(('groups', 'rows'), 'heads'), parts along dimension 0
The draws below stay inside these ranges and needn't reach their ends.
There are 2 independent parts, one for each index of `groups`. The reference program is written for one: setup_inputs(seed, part) draws one part's arguments, and reference() takes and returns one part's arrays. A program takes and returns all parts, laid end to end along the dimension named above; an argument that names none is the same for every part. Nothing has to cross between parts.
Inputs may be any that keep to these rules, and one draw needn't show every extreme that they name: `expert_ids`: every row names 10 different experts. In each aligned block of 20 rows no expert is named more than 8 times, a bound that some block reaches.
All inputs are finite; a program needn't handle non-finite values.
Results may differ from the reference program's by a relative error of at most 0.0034.
Values may be sent and summed in bfloat16 or wider, within the bound.
No kernel may reach another device: no remote copies, remote signals or barrier semaphores. Data moves between devices by JAX's collectives and lax.ppermute only.
A program may use at most 64 MiB of HBM per device.

```python
import math
import jax
import jax.numpy as jnp
import numpy as np
from jax import lax

D = 2048
VH = 16
QH = 8
DK = 128
DV = 128
EH = 256
TOPK = 10
DRAFT = 4
REQ_DEV = 5
E = 32
CAP = 8
REQUESTS = 80
TOKENS = 320
N_ROWS = 16


def column_scales(low, high):
    position = jnp.arange(D, dtype=jnp.float32) / (D - 1)
    return low * jnp.exp(position * jnp.log(high / low))


def draw_residual(key, part):
    key = jax.random.fold_in(key, 11)
    noise = jax.random.truncated_normal(key, -5.5, 5.5, (TOKENS, D), jnp.float32)
    scales = column_scales(0.4, 2.0)
    return (noise * scales[None, :]).astype(jnp.bfloat16)


def plant(values, key, least, high):
    shape = values.shape
    index_at = [jax.random.randint(jax.random.fold_in(key, axis), (), 0, shape[axis]) for axis in range(len(shape))]
    values = values.at[tuple(index_at)].set(least)
    longest = shape.index(max(shape))
    index_at[longest] = (index_at[longest] + 1) % shape[longest]
    return values.at[tuple(index_at)].set(high)


def block_scale(rng, shape, shards, low, high):
    factor_of, own = 1.0, jax.random.fold_in(rng, 6)
    for axis_at, parts in shards:
        steps = jnp.exp(jax.random.uniform(jax.random.fold_in(own, axis_at), (parts,), jnp.float32, low / len(shards), high / len(shards)))
        factor_of = factor_of * jnp.repeat(steps, shape[axis_at] // parts).reshape([-1 if axis == axis_at else 1 for axis in range(len(shape))])
    return factor_of


def assign_block(stream_key, own, number, rows, count, top, limit, lean):
    sequence = jax.random.permutation(stream_key, count)
    crowded, common = portions_of(count, rows * top, limit, lean, True), portions_of(count, rows * top, limit, lean, False)
    places = jnp.arange(count)

    def named(lengths, rotation):
        used = int((lengths > 0).sum())
        fixed = max(1, used // 4)
        moved = fixed + (places - fixed + rotation * (used - fixed)) % max(1, count - fixed)
        return jnp.zeros((count,), jnp.int32).at[sequence[jnp.where(places < fixed, places, moved)]].set(jnp.asarray(lengths, jnp.int32))

    lengths = jnp.where(number % 4 == 0, named(crowded, number // 4), named(common, number - number // 4 - 1))
    mixed = jax.random.permutation(jax.random.fold_in(own, 3), count)
    donor, sink = mixed[0:count // 2 * 2:2], mixed[1:count // 2 * 2:2]
    slack = jnp.minimum(lengths[donor] - 1, limit - lengths[sink]) // 2
    slack = jnp.where((donor == sequence[0]) | (sink == sequence[0]) | (lengths[sink] == 0), 0, jnp.maximum(slack, 0))
    moved = jax.random.randint(jax.random.fold_in(own, 4), (count // 2,), 0, 1 << 20) % (slack + 1)
    lengths = lengths.at[donor].add(-moved).at[sink].add(moved)
    labels = jnp.searchsorted(jnp.cumsum(lengths), jnp.arange(rows * top), side="right").astype(jnp.int32)
    table = labels.reshape(top, rows).T
    table = table[jax.random.permutation(jax.random.fold_in(own, 1), rows)]
    rotation = jax.random.randint(jax.random.fold_in(own, 2), (rows, 1), 0, top)
    return jnp.take_along_axis(table, (jnp.arange(top)[None, :] + rotation) % top, axis=1)


def portions_of(count, total, reach, lean, full):
    weights = [(1 << 20) // math.isqrt(rank ** lean) + 1 for rank in range(1, count + 1)]
    largest = reach if full else min(reach, max(-(-total // count), total * weights[0] // sum(weights)))
    least = 1 if total - largest >= count - 1 else 0
    holding, spare = [largest] + [least] * (count - 1), total - largest - least * (count - 1)
    while spare > 0:
        candidates = [i for i in range(1, count) if holding[i] < largest] or [i for i in range(1, count) if holding[i] < reach]
        whole, budget = sum([weights[i] for i in candidates]), spare
        for i in candidates:
            addition = min(reach - holding[i], max(1, budget * weights[i] // whole), spare)
            holding[i] = holding[i] + addition
            spare = spare - addition
    return np.array(holding)


def gaussian(stream_key, shape, spread, limit, pieces=(), held_as=jnp.bfloat16):
    level = block_scale(stream_key, shape, pieces, -0.22, 0.18) if pieces else 1.0
    array = jax.random.normal(stream_key, shape, jnp.float32) * spread * level
    return jnp.minimum(jnp.maximum(array, -limit), limit).astype(held_as)


def setup_inputs(seed: int = 0, part: int = 0) -> dict:
    key_list = jax.random.split(jax.random.key(seed), 19)
    part_keys = jax.random.split(jax.random.fold_in(key_list[18], part), 19)
    query_in = gaussian(part_keys[0], (TOKENS, QH * DK), 1.0, 6.0, ((0, 16),))
    key_in = gaussian(part_keys[1], (TOKENS, QH * DK), 1.0, 6.0, ((0, 16),))
    value_in = gaussian(part_keys[2], (TOKENS, VH * DV), 1.0, 6.0, ((0, 16),))
    gate_in = gaussian(part_keys[3], (TOKENS, VH * DV), 1.0, 6.0, ((0, 16),))
    decay_in = gaussian(part_keys[4], (TOKENS, VH), 1.0, 6.0, ((0, 16),), jnp.float32)
    beta_in = gaussian(part_keys[5], (TOKENS, VH), 1.5, 6.0, ((0, 16),), jnp.float32)
    decay_rate = jnp.clip(jnp.exp(jax.random.uniform(key_list[6], (VH,), jnp.float32, math.log(0.02), math.log(4.0))), 0.02, 4.0)
    decay_bias = jnp.clip(jax.random.uniform(key_list[7], (VH,), jnp.float32, -1.0, 1.0), -1.0, 1.0)
    norm_gain = jnp.clip(1.0 + 0.1 * jax.random.normal(key_list[8], (DV,), jnp.float32), 0.5, 1.5)
    prior_state = gaussian(part_keys[9], (REQUESTS, VH, DK, DV), 0.3, 4.0, ((0, 16),))
    accepted = plant(jax.random.randint(part_keys[10], (REQUESTS,), 1, DRAFT + 1), jax.random.fold_in(part_keys[10], 1), 1, DRAFT).astype(jnp.int32)
    out_weight = gaussian(key_list[11], (VH * DV, D), (VH * DV) ** -0.5, 0.125, ((1, 16),))
    residual = draw_residual(jax.random.fold_in(jax.random.fold_in(key_list[18], part), 71), part)
    post_gain = jnp.clip(1.0 + 0.1 * jax.random.normal(key_list[13], (D,), jnp.float32), 0.5, 1.5)
    expert_ids_keys = jax.random.split(jax.random.fold_in(part_keys[14], 1), TOKENS // (REQ_DEV * DRAFT))
    expert_ids_turns = jax.random.permutation(jax.random.fold_in(part_keys[14], 3), TOKENS // (REQ_DEV * DRAFT))
    expert_ids = jax.vmap(lambda own, number: assign_block(jax.random.fold_in(part_keys[14], 2), own, number, REQ_DEV * DRAFT, E, TOPK, CAP, 2))(expert_ids_keys, expert_ids_turns).reshape((TOKENS, TOPK))
    expert_scores = jnp.clip(jnp.exp(math.log(1.0) - 2.3025851 * jax.random.uniform(part_keys[15], (TOKENS, TOPK), jnp.float32) ** block_scale(part_keys[15], (TOKENS, TOPK), ((0, 16),), -0.2, 0.2)), 0.1, 1.0)
    expert_up = gaussian(key_list[16], (E, D, 2 * EH), D ** -0.5, 0.125, ((0, 16),))
    expert_down = gaussian(key_list[17], (E, EH, D), EH ** -0.5, 0.375, ((0, 16),))
    return {"query_in": query_in, "key_in": key_in, "value_in": value_in, "gate_in": gate_in, "decay_in": decay_in, "beta_in": beta_in, "decay_rate": decay_rate, "decay_bias": decay_bias, "norm_gain": norm_gain, "prior_state": prior_state, "accepted": accepted, "out_weight": out_weight, "residual": residual, "post_gain": post_gain, "expert_ids": expert_ids, "expert_scores": expert_scores, "expert_up": expert_up, "expert_down": expert_down}


EPS = 1e-06
HIGH = lax.Precision.HIGHEST

def unit_rows(values_in, width):
    shaped = values_in.reshape(values_in.shape[0], -1, width)
    return shaped * lax.rsqrt(lax.optimization_barrier(jnp.sum(shaped * shaped, axis=-1, keepdims=True)) + EPS)

def delta_rule(query_in, key_in, value_in, gate_in, decay_in, beta_in, decay_rate, decay_bias, norm_gain, prior_state, accepted):
    tok_rows = query_in.shape[0]
    req_rows, heads_here, key_width, value_width = prior_state.shape
    drafts = tok_rows // req_rows
    repeat_by = heads_here // (query_in.shape[1] // key_width)
    queries = jnp.repeat(unit_rows(query_in.astype(jnp.float32), key_width), repeat_by, axis=1) * key_width ** (-0.5)
    keys_all = jnp.repeat(unit_rows(key_in.astype(jnp.float32), key_width), repeat_by, axis=1)
    values_all = value_in.astype(jnp.float32).reshape(tok_rows, heads_here, value_width)
    queries = queries.reshape(req_rows, drafts, heads_here, key_width)
    keys_all = keys_all.reshape(req_rows, drafts, heads_here, key_width)
    values_all = values_all.reshape(req_rows, drafts, heads_here, value_width)
    log_decay = -decay_rate * jax.nn.softplus(decay_in + decay_bias)
    log_decay = log_decay.reshape(req_rows, drafts, heads_here)
    beta_rate = jax.nn.sigmoid(beta_in).reshape(req_rows, drafts, heads_here)
    carried = prior_state.astype(jnp.float32)
    held = carried
    readouts = []
    for draft_step in range(drafts):
        carried = carried * jnp.exp(log_decay[:, draft_step])[:, :, None, None]
        memory = jnp.einsum('rhk,rhkv->rhv', keys_all[:, draft_step], carried, precision=HIGH)
        delta_term = (values_all[:, draft_step] - memory) * beta_rate[:, draft_step][:, :, None]
        carried = carried + keys_all[:, draft_step][..., None] * delta_term[:, :, None, :]
        readouts.append(jnp.einsum('rhk,rhkv->rhv', queries[:, draft_step], carried, precision=HIGH))
        held = jnp.where((accepted == draft_step + 1)[:, None, None, None], carried, held)
    readout = jnp.stack(readouts, axis=1).reshape(tok_rows, heads_here, value_width)
    inv_norm = lax.rsqrt(lax.optimization_barrier(jnp.mean(readout * readout, axis=-1, keepdims=True)) + EPS)
    gating = jax.nn.silu(gate_in.astype(jnp.float32).reshape(tok_rows, heads_here, value_width))
    mixed_heads = (readout * inv_norm * norm_gain * gating).astype(jnp.bfloat16)
    return (mixed_heads.reshape(tok_rows, heads_here * value_width), held.astype(jnp.bfloat16))

def reference(query_in, key_in, value_in, gate_in, decay_in, beta_in, decay_rate, decay_bias, norm_gain, prior_state, accepted, out_weight, residual, post_gain, expert_ids, expert_scores, expert_up, expert_down):
    mixed_heads, kept_state = delta_rule(query_in, key_in, value_in, gate_in, decay_in, beta_in, decay_rate, decay_bias, norm_gain, prior_state, accepted)
    attention = jnp.dot(mixed_heads, out_weight, preferred_element_type=jnp.float32)
    hidden_sum = residual.astype(jnp.float32) + attention
    inv_rms = lax.rsqrt(lax.optimization_barrier(jnp.mean(hidden_sum * hidden_sum, axis=1, keepdims=True)) + EPS)
    normed = (hidden_sum * inv_rms * post_gain).astype(jnp.bfloat16)
    block_ids = expert_ids.reshape(N_ROWS, -1)
    onehot = (block_ids[:, :, None] == jnp.arange(E, dtype=jnp.int32)[None, None, :]).astype(jnp.int32)
    earlier = jnp.cumsum(onehot, axis=1) - onehot
    slot_index = lax.optimization_barrier(jnp.sum(earlier * onehot, axis=2))
    source_rows = jnp.arange(N_ROWS, dtype=jnp.int32)[:, None]
    position = (block_ids * (N_ROWS * CAP) + source_rows * CAP + slot_index).reshape(-1)
    token_index = jnp.repeat(jnp.arange(TOKENS, dtype=jnp.int32), TOPK)
    slot_table = jnp.zeros((E * N_ROWS * CAP,), jnp.int32).at[position].set(token_index)

    def run_expert(inputs):
        picked, up_part, down_part = inputs
        rows_in = normed[picked]
        full_up = jnp.dot(rows_in, up_part, preferred_element_type=jnp.float32)
        activation = (jax.nn.silu(full_up[:, :EH]) * full_up[:, EH:]).astype(jnp.bfloat16)
        return jnp.dot(activation, down_part, preferred_element_type=jnp.float32).astype(jnp.bfloat16)
    outputs = lax.map(run_expert, (slot_table.reshape(E, N_ROWS * CAP), expert_up, expert_down))
    values_back = outputs.reshape(-1, D)[position].astype(jnp.float32).reshape(TOKENS, TOPK, D)
    weights = expert_scores / lax.optimization_barrier(jnp.sum(expert_scores, axis=1, keepdims=True))
    layer_out = (hidden_sum + lax.optimization_barrier(jnp.sum(weights[:, :, None] * values_back, axis=1))).astype(jnp.bfloat16)
    return (layer_out, kept_state)
```

```python
import functools

import jax
import jax.numpy as jnp
from jax import lax
from jax.experimental import pallas as pl
from jax.experimental.pallas import tpu as pltpu
from jax.sharding import PartitionSpec as P

EPS = 1e-06
BF16 = jnp.bfloat16
F32 = jnp.float32


def round_up(value, step):
    return -(-value // step) * step


def delta_kernel(
    drafts,
    group,
    accepted_ref,
    query_ref,
    key_ref,
    value_ref,
    gate_ref,
    decay_ref,
    beta_ref,
    rate_ref,
    bias_ref,
    gain_ref,
    state_ref,
    mixed_ref,
    kept_ref,
    coef,
    unit,
    vals,
):
    step = pl.program_id(0)
    tok = query_ref.shape[0]
    pad = coef.shape[1]
    reqs, _, width, vwidth = state_ref.shape
    repeat = state_ref.shape[1] // group

    def shift(values, by):
        return pltpu.roll(values, by % pad, 0) if by % pad else values

    @pl.when(step == 0)
    def _():
        heads = decay_ref.shape[1]
        coef[...] = jnp.zeros_like(coef)
        unit[...] = jnp.zeros_like(unit)
        vals[...] = jnp.zeros_like(vals)
        at = lax.broadcasted_iota(jnp.int32, (pad, heads), 0)
        draft = at % drafts
        left = jnp.zeros_like(at)
        for r in range(reqs):
            left = jnp.where(at // drafts == r, accepted_ref[r], left)
        left = left - 1 - draft
        coef[0, 0:tok, :] = -rate_ref[...] * jax.nn.softplus(decay_ref[...] + bias_ref[...])
        coef[1, 0:tok, :] = jax.nn.sigmoid(beta_ref[...])
        log_decay = coef[0]
        sums = [jnp.zeros_like(log_decay)]
        for o in range(drafts):
            sums.append(sums[-1] + shift(log_decay, o))
        total = sums[1]
        for s in range(1, drafts):
            total = jnp.where(draft == s, sums[s + 1], total)
        coef[0] = jnp.exp(total)
        for o in range(1, drafts):
            coef[1 + o] = jnp.where(draft >= o, jnp.exp(sums[o]), 0.0)
        ahead = jnp.zeros_like(log_decay)
        later = jnp.zeros_like(log_decay)
        for o in range(1, drafts):
            ahead = ahead + shift(log_decay, -o)
            later = jnp.where(left == o, ahead, later)
        coef[1 + drafts] = jnp.where(left >= 0, jnp.exp(later), 0.0)
        coef[2 + drafts] = jnp.exp(total + later)

    lane = lax.broadcasted_iota(jnp.int32, coef.shape[1:], 1)
    row = lax.broadcasted_iota(jnp.int32, (2 * pad, width), 0)
    request = row % pad // drafts
    row3 = lax.broadcasted_iota(jnp.int32, (3 * pad, width), 0)
    request3 = row3 % pad // drafts
    for i in range(group):
        cols = slice(i * width, (i + 1) * width)
        for slot, ref, factor in ((0, query_ref, width ** (-0.5)), (1, key_ref, 1.0)):
            raw = ref[:, cols].astype(F32)
            scale = lax.rsqrt(jnp.sum(raw * raw, axis=1, keepdims=True) + EPS) * factor
            unit[i, slot * pad : slot * pad + tok, :] = raw * scale
        both = unit[i]
        high = both.astype(BF16).astype(F32)
        low = both - high
        spread = []
        for r in range(reqs):
            part = request == r
            spread.append(
                jnp.concatenate(
                    [jnp.where(part, high, 0.0), jnp.where(part, low, 0.0)], axis=0
                ).astype(BF16)
            )
        spread = jnp.concatenate(spread, axis=1)
        prior = jnp.concatenate(
            [
                jnp.concatenate([state_ref[r, repeat * i + j] for j in range(repeat)], axis=1)
                for r in range(reqs)
            ],
            axis=0,
        )
        read = jnp.dot(spread, prior, preferred_element_type=F32)
        query_prior = read[0:pad] + read[2 * pad : 3 * pad]
        key_prior = read[pad : 2 * pad] + read[3 * pad : 4 * pad]
        query, key = both[0:pad], both[pad : 2 * pad]
        shifted = [shift(key, o) for o in range(drafts)]
        query_key = [jnp.sum(query * s, axis=1, keepdims=True) for s in shifted]
        key_key = [jnp.sum(key * s, axis=1, keepdims=True) for s in shifted]
        written = []
        keeps = []
        for j in range(repeat):
            head = (step * group + i) * repeat + j
            vcols = slice((repeat * i + j) * vwidth, (repeat * i + j + 1) * vwidth)
            at = slice(j * vwidth, (j + 1) * vwidth)

            def column(index):
                return jnp.sum(jnp.where(lane == head, coef[index], 0.0), axis=1, keepdims=True)

            through, rate = column(0), column(1)
            decays = [column(1 + o) for o in range(1, drafts)]
            vals[j, 0:tok, :] = value_ref[:, vcols].astype(F32)
            base = rate * (vals[j] - through * key_prior[:, at])
            mixes = [rate * decays[o - 1] * key_key[o] for o in range(1, drafts)]
            delta = base
            for _ in range(1, drafts):
                delta = base - sum(mixes[o - 1] * shift(delta, o) for o in range(1, drafts))
            out = through * query_prior[:, at] + query_key[0] * delta
            for o in range(1, drafts):
                out = out + (decays[o - 1] * query_key[o]) * shift(delta, o)
            norm = lax.rsqrt(jnp.mean(out * out, axis=1, keepdims=True) + EPS)
            gate = gate_ref[:, vcols].astype(F32)
            mixed = (out * norm)[0:tok] * gain_ref[...] * jax.nn.silu(gate)
            mixed_ref[:, vcols] = mixed.astype(BF16)
            written.append(column(1 + drafts) * delta)
            keeps.append(jnp.broadcast_to(column(2 + drafts), (pad, vwidth)))
        written = jnp.concatenate(written, axis=1)
        whigh = written.astype(BF16).astype(F32)
        wlow = written - whigh
        wrote = jnp.concatenate([whigh, wlow, whigh], axis=0).astype(BF16)
        kcat = jnp.concatenate([high[pad:], high[pad:], low[pad:]], axis=0)
        kspread = jnp.concatenate(
            [jnp.where(request3 == r, kcat, 0.0).astype(BF16) for r in range(reqs)], axis=1
        )
        update = lax.dot_general(
            kspread, wrote, (((0,), (0,)), ((), ())), preferred_element_type=F32
        )
        for r in range(reqs):
            for j in range(repeat):
                keep = keeps[j][r * drafts : r * drafts + 1, :]
                kept_ref[r, repeat * i + j] = (
                    keep * state_ref[r, repeat * i + j].astype(F32)
                    + update[r * width : (r + 1) * width, j * vwidth : (j + 1) * vwidth]
                ).astype(BF16)


def delta_rule(
    query_in,
    key_in,
    value_in,
    gate_in,
    decay_in,
    beta_in,
    decay_rate,
    decay_bias,
    norm_gain,
    prior_state,
    accepted,
):
    tok = query_in.shape[0]
    reqs, heads, width, vwidth = prior_state.shape
    drafts = tok // reqs
    query_heads = query_in.shape[1] // width
    repeat = heads // query_heads
    group = 2 if query_heads % 2 == 0 else 1
    pad = round_up(tok, 8)
    whole = lambda *shape: pl.BlockSpec(shape, lambda g: (0,) * len(shape))
    qblock = pl.BlockSpec((tok, group * width), lambda g: (0, g))
    vblock = pl.BlockSpec((tok, group * repeat * vwidth), lambda g: (0, g))
    sblock = pl.BlockSpec((reqs, group * repeat, width, vwidth), lambda g: (0, g, 0, 0))
    return pl.pallas_call(
        functools.partial(delta_kernel, drafts, group),
        grid=(query_heads // group,),
        in_specs=[
            pl.BlockSpec(memory_space=pltpu.SMEM),
            qblock,
            qblock,
            vblock,
            vblock,
            whole(tok, heads),
            whole(tok, heads),
            whole(1, heads),
            whole(1, heads),
            whole(1, vwidth),
            sblock,
        ],
        out_specs=[vblock, sblock],
        out_shape=[
            jax.ShapeDtypeStruct((tok, heads * vwidth), BF16),
            jax.ShapeDtypeStruct(prior_state.shape, BF16),
        ],
        scratch_shapes=[
            pltpu.VMEM((3 + drafts, pad, heads), F32),
            pltpu.VMEM((group, 2 * pad, width), F32),
            pltpu.VMEM((repeat, pad, vwidth), F32),
        ],
        compiler_params=pltpu.CompilerParams(vmem_limit_bytes=32 * 1024 * 1024),
        cost_estimate=pl.CostEstimate(
            flops=4 * heads * reqs * width * vwidth * 96,
            bytes_accessed=4 * heads * reqs * width * vwidth,
            transcendentals=0,
        ),
    )(
        accepted,
        query_in,
        key_in,
        value_in,
        gate_in,
        decay_in,
        beta_in,
        decay_rate.reshape(1, heads),
        decay_bias.reshape(1, heads),
        norm_gain.reshape(1, vwidth),
        prior_state,
    )


def swap(values, mask):
    count = lax.axis_size("rows")
    return lax.ppermute(values, "rows", [(i, i ^ mask) for i in range(count)])


def routing(expert_ids, expert_scores, experts):
    weights = expert_scores / jnp.sum(expert_scores, axis=1, keepdims=True)
    named = expert_ids[:, :, None] == jnp.arange(experts, dtype=jnp.int32)
    dense = jnp.sum(jnp.where(named, weights[:, :, None], 0.0), axis=1)
    high = dense.astype(BF16)
    low = (dense - high.astype(F32)).astype(BF16)
    return jnp.concatenate([high, low], axis=1)


def run_experts(tokens, routes, ups, downs, numbers, experts):
    total = None
    for up, down, number in zip(ups, downs, numbers):
        inner = down.shape[0]
        full = jnp.dot(tokens, up, preferred_element_type=F32)
        here = lax.dynamic_slice(routes, (0, number), (routes.shape[0], 1)).astype(F32)
        rest = lax.dynamic_slice(routes, (0, experts + number), (routes.shape[0], 1)).astype(F32)
        act = jax.nn.silu(full[:, :inner]) * full[:, inner:] * (here + rest)
        term = jnp.dot(act.astype(BF16), down, preferred_element_type=F32)
        total = term if total is None else total + term
    return total


def plane_layer(
    mixed,
    out_weight,
    residual,
    post_gain,
    expert_ids,
    expert_scores,
    expert_up,
    expert_down,
):
    count = lax.axis_size("rows")
    line = count // 4
    me = lax.axis_index("rows")
    here = me // 4
    others = range(1, line)
    tok, full = residual.shape
    exp_dev = expert_up.shape[0]
    experts = exp_dev * count
    part = full // line

    weight_x = swap(out_weight, 2)
    up_mate = swap(expert_up, 1)
    down_mate = swap(expert_down, 1)
    weights = [out_weight, swap(out_weight, 1), weight_x, swap(weight_x, 1)]
    projection = jnp.zeros((out_weight.shape[0], part), BF16)
    for mask, piece in enumerate(weights):
        projection = lax.dynamic_update_slice(
            projection, piece, (0, ((me % 4) ^ mask) * piece.shape[1])
        )

    routes = routing(expert_ids, expert_scores, experts)
    own_res = [
        lax.dynamic_slice(residual, (0, (here ^ m) * part), (tok, part)) for m in range(line)
    ]
    packed = [jnp.concatenate([mixed, own_res[m], routes], axis=1) for m in range(line)]
    got = [packed[0]] + [swap(packed[m], 4 * m) for m in others]
    got = jnp.concatenate(got, axis=0)
    width = mixed.shape[1]
    hidden = got[:, width : width + part].astype(F32) + jnp.dot(
        got[:, :width], projection, preferred_element_type=F32
    )
    hidden = hidden.astype(BF16)
    routes = got[:, width + part :]

    hid = jnp.zeros((line * tok, full), BF16)
    for m in range(line):
        piece = hidden if m == 0 else swap(hidden, 4 * m)
        piece = jnp.concatenate([piece[tok * (j ^ m) : tok * (j ^ m) + tok] for j in range(line)], axis=0)
        hid = lax.dynamic_update_slice(hid, piece, (0, (here ^ m) * part))
    hid = hid.astype(F32)
    scale = lax.rsqrt(jnp.mean(hid * hid, axis=1, keepdims=True) + EPS)
    normed = (hid * scale * post_gain).astype(BF16)

    sent = jnp.concatenate([normed, routes], axis=1)
    came = swap(sent, 2)
    ups = [expert_up[i] for i in range(exp_dev)] + [up_mate[i] for i in range(exp_dev)]
    downs = [expert_down[i] for i in range(exp_dev)] + [down_mate[i] for i in range(exp_dev)]
    numbers = [me * exp_dev + i for i in range(exp_dev)] + [(me ^ 1) * exp_dev + i for i in range(exp_dev)]
    own_sum = run_experts(normed, routes, ups, downs, numbers, experts)
    far_sum = run_experts(came[:, :full], came[:, full:], ups, downs, numbers, experts)
    back = swap(far_sum.astype(BF16), 2)
    total = own_sum + back.astype(F32)
    out = hid[:tok] + total[:tok]
    for m in others:
        out = out + swap(total[m * tok : (m + 1) * tok].astype(BF16), 4 * m).astype(F32)
    return out.astype(BF16)


def general_layer(
    mixed,
    out_weight,
    residual,
    post_gain,
    expert_ids,
    expert_scores,
    expert_up,
    expert_down,
):
    partial_value = jnp.dot(
        mixed,
        lax.all_gather(out_weight, "rows", axis=1, tiled=True),
        preferred_element_type=F32,
    )
    attention = lax.psum_scatter(partial_value, "heads", scatter_dimension=1, tiled=True)
    hidden_sum = residual.astype(F32) + attention
    full_width = residual.shape[1] * lax.axis_size("heads")
    square = lax.psum(jnp.sum(hidden_sum * hidden_sum, axis=1), "heads")
    inv_rms = lax.rsqrt(square / full_width + EPS)
    normed = (hidden_sum * inv_rms[:, None] * post_gain).astype(BF16)
    tok_rows, top_count = expert_ids.shape
    row_count = lax.axis_size("rows")
    exp_dev = expert_up.shape[0]
    experts_all = exp_dev * row_count
    capacity = max(2, (tok_rows * top_count + experts_all - 1) // experts_all + 1)
    half_width = normed.shape[1]
    flat_ids = expert_ids.reshape(-1)
    onehot = (flat_ids[:, None] == jnp.arange(experts_all, dtype=jnp.int32)[None, :]).astype(
        jnp.int32
    )
    earlier = jnp.cumsum(onehot, axis=0) - onehot
    slot_index = jnp.sum(earlier * onehot, axis=1)
    position = (flat_ids % exp_dev * row_count + flat_ids // exp_dev) * capacity + slot_index
    select = (
        jnp.arange(experts_all * capacity, dtype=jnp.int32)[:, None] == position[None, :]
    ).astype(BF16)
    spread = jnp.repeat(normed, top_count, axis=0)
    outgoing = jnp.dot(select, spread, preferred_element_type=F32).astype(BF16)
    outgoing = outgoing.reshape(exp_dev, row_count, capacity, half_width)
    arrived = lax.all_to_all(outgoing, "rows", split_axis=1, concat_axis=1, tiled=True)
    rows_in = arrived.reshape(exp_dev, row_count * capacity, half_width)
    partial_up = jnp.einsum("lnd,ldf->lnf", rows_in, expert_up, preferred_element_type=F32)
    full_up = lax.psum(partial_up, "heads")
    inner_width = expert_down.shape[1]
    activation = (jax.nn.silu(full_up[..., :inner_width]) * full_up[..., inner_width:]).astype(BF16)
    result = jnp.einsum("lnf,lfd->lnd", activation, expert_down, preferred_element_type=F32)
    returned = lax.all_to_all(
        result.astype(BF16).reshape(exp_dev, row_count, capacity, half_width),
        "rows",
        split_axis=1,
        concat_axis=1,
        tiled=True,
    )
    values_back = jnp.dot(select.T, returned.reshape(-1, half_width), preferred_element_type=F32)
    values_back = values_back.reshape(tok_rows, top_count, half_width)
    weights = expert_scores / jnp.sum(expert_scores, axis=1, keepdims=True)
    return (hidden_sum + jnp.sum(weights[:, :, None] * values_back, axis=1)).astype(BF16)


def per_device(mesh_shape, *args):
    delta_args, layer_args = args[:11], args[11:]
    mixed, kept_state = delta_rule(*delta_args)
    short = mesh_shape["heads"] == 1 and mesh_shape["rows"] in (8, 16)
    layer = plane_layer if short else general_layer
    return (layer(mixed, *layer_args), kept_state)


def solution(mesh):
    return jax.shard_map(
        functools.partial(per_device, dict(mesh.shape)),
        mesh=mesh,
        in_specs=(
            P(("groups", "rows"), "heads"),
            P(("groups", "rows"), "heads"),
            P(("groups", "rows"), "heads"),
            P(("groups", "rows"), "heads"),
            P(("groups", "rows"), "heads"),
            P(("groups", "rows"), "heads"),
            P("heads"),
            P("heads"),
            P(),
            P(("groups", "rows"), "heads", None, None),
            P(("groups", "rows")),
            P("heads", "rows"),
            P(("groups", "rows"), "heads"),
            P("heads"),
            P(("groups", "rows"), None),
            P(("groups", "rows"), None),
            P("rows", "heads", None),
            P("rows", None, "heads"),
        ),
        out_specs=(P(("groups", "rows"), "heads"), P(("groups", "rows"), "heads", None, None)),
        check_vma=False,
    )
```

```python
import functools

import jax
import jax.numpy as jnp
from jax import lax
from jax.experimental import pallas as pl
from jax.experimental.pallas import tpu as pltpu
from jax.sharding import PartitionSpec as P

EPS = 1e-06
BF16 = jnp.bfloat16
F32 = jnp.float32


def round_up(value, step):
    return -(-value // step) * step


def delta_kernel(
    drafts,
    group,
    line,
    accepted_ref,
    query_ref,
    key_ref,
    value_ref,
    gate_ref,
    decay_ref,
    beta_ref,
    rate_ref,
    bias_ref,
    gain_ref,
    state_ref,
    *refs,
):
    if line:
        residual_ref, ids_ref, scores_ref = refs[:3]
        packed_refs, refs = refs[3 : 3 + line], refs[3 + line :]
        kept_ref, coef, unit, vals, mixed_ref, pack = refs
    else:
        mixed_ref, kept_ref, coef, unit, vals = refs
    step = pl.program_id(0)
    tok = query_ref.shape[0]
    pad = unit.shape[1] // 2
    reqs, _, width, vwidth = state_ref.shape
    repeat = state_ref.shape[1] // group
    heads = decay_ref.shape[0]

    def shift(values, by):
        return pltpu.roll(values, by % pad, 0) if by % pad else values

    def ahead_of(values, by):
        return pltpu.roll(values, by % 128, 1) if by % 128 else values

    @pl.when(step == 0)
    def _():
        unit[...] = jnp.zeros_like(unit)
        vals[...] = jnp.zeros_like(vals)
        coef[...] = jnp.zeros_like(coef)
        square = (heads, heads)
        eye = lax.broadcasted_iota(jnp.int32, square, 0) == lax.broadcasted_iota(jnp.int32, square, 1)
        rate = jnp.sum(jnp.where(eye, rate_ref[...], 0.0), axis=1, keepdims=True)
        bias = jnp.sum(jnp.where(eye, bias_ref[...], 0.0), axis=1, keepdims=True)
        coef[0:heads, 0:tok] = -rate * jax.nn.softplus(decay_ref[...] + bias)
        coef[heads : 2 * heads, 0:tok] = jax.nn.sigmoid(beta_ref[...])
        log_decay = coef[0:heads]
        at = lax.broadcasted_iota(jnp.int32, log_decay.shape, 1)
        draft = at % drafts
        left = jnp.zeros_like(at)
        for r in range(reqs):
            left = jnp.where(at // drafts == r, accepted_ref[r], left)
        left = left - 1 - draft
        sums = [jnp.zeros_like(log_decay)]
        for o in range(drafts):
            sums.append(sums[-1] + ahead_of(log_decay, o))
        total = sums[1]
        for s in range(1, drafts):
            total = jnp.where(draft == s, sums[s + 1], total)
        coef[0:heads] = jnp.exp(total)
        for o in range(1, drafts):
            coef[(1 + o) * heads : (2 + o) * heads] = jnp.where(draft >= o, jnp.exp(sums[o]), 0.0)
        ahead = jnp.zeros_like(log_decay)
        later = jnp.zeros_like(log_decay)
        for o in range(1, drafts):
            ahead = ahead + ahead_of(log_decay, -o)
            later = jnp.where(left == o, ahead, later)
        coef[(1 + drafts) * heads : (2 + drafts) * heads] = jnp.where(
            left >= 0, jnp.exp(later), 0.0
        )
        coef[(2 + drafts) * heads : (3 + drafts) * heads] = jnp.exp(total + later)
        coef[...] = coef[...].T
        if line:
            rows = pack.shape[0] // 2
            half = mixed_ref.shape[1] // 2
            scores = scores_ref[...]
            scores = scores / jnp.sum(scores, axis=0, keepdims=True)
            experts = 64
            number = lax.broadcasted_iota(jnp.int32, (experts, tok), 0)
            dense = jnp.zeros((experts, tok), F32)
            for k in range(ids_ref.shape[0]):
                dense = dense + jnp.where(number == ids_ref[k : k + 1, :], scores[k : k + 1], 0.0)
            high = dense.astype(BF16).astype(F32)
            routes = jnp.concatenate([high, dense - high], axis=0)
            routes = jnp.concatenate(
                [routes, jnp.zeros((2 * experts, 128 - tok), F32)], axis=1
            ).T
            pack[...] = jnp.zeros_like(pack)
            part = mixed_ref.shape[1] // line
            at = half + part - (pack.shape[1] - half)
            pack[rows : 2 * rows, at : at + 128] = routes[0:tok]

    lane = lax.broadcasted_iota(jnp.int32, (pad, coef.shape[1]), 1)
    row = lax.broadcasted_iota(jnp.int32, (2 * pad, width), 0)
    request = row % pad // drafts
    row3 = lax.broadcasted_iota(jnp.int32, (3 * pad, width), 0)
    request3 = row3 % pad // drafts
    for i in range(group):
        cols = slice(i * width, (i + 1) * width)
        for slot, ref, factor in ((0, query_ref, width ** (-0.5)), (1, key_ref, 1.0)):
            raw = ref[:, cols].astype(F32)
            scale = lax.rsqrt(jnp.sum(raw * raw, axis=1, keepdims=True) + EPS) * factor
            unit[i, slot * pad : slot * pad + tok, :] = raw * scale
        both = unit[i]
        high = both.astype(BF16).astype(F32)
        low = both - high
        spread = []
        for r in range(reqs):
            part = request == r
            spread.append(
                jnp.concatenate(
                    [jnp.where(part, high, 0.0), jnp.where(part, low, 0.0)], axis=0
                ).astype(BF16)
            )
        spread = jnp.concatenate(spread, axis=1)
        prior = jnp.concatenate(
            [
                jnp.concatenate([state_ref[r, repeat * i + j] for j in range(repeat)], axis=1)
                for r in range(reqs)
            ],
            axis=0,
        )
        read = jnp.dot(spread, prior, preferred_element_type=F32)
        query_prior = read[0:pad] + read[2 * pad : 3 * pad]
        key_prior = read[pad : 2 * pad] + read[3 * pad : 4 * pad]
        query, key = both[0:pad], both[pad : 2 * pad]
        shifted = [shift(key, o) for o in range(drafts)]
        query_key = [jnp.sum(query * s, axis=1, keepdims=True) for s in shifted]
        key_key = [jnp.sum(key * s, axis=1, keepdims=True) for s in shifted]
        written = []
        keeps = []
        for j in range(repeat):
            head = (step * group + i) * repeat + j
            vcols = slice((repeat * i + j) * vwidth, (repeat * i + j + 1) * vwidth)
            at = slice(j * vwidth, (j + 1) * vwidth)

            def column(index):
                mine = jnp.where(lane == index * heads + head, coef[0:pad], 0.0)
                return jnp.sum(mine, axis=1, keepdims=True)

            through, rate = column(0), column(1)
            decays = [column(1 + o) for o in range(1, drafts)]
            vals[j, 0:tok, :] = value_ref[:, vcols].astype(F32)
            base = rate * (vals[j] - through * key_prior[:, at])
            mixes = [rate * decays[o - 1] * key_key[o] for o in range(1, drafts)]
            delta = base
            for _ in range(1, drafts):
                delta = base - sum(mixes[o - 1] * shift(delta, o) for o in range(1, drafts))
            out = through * query_prior[:, at] + query_key[0] * delta
            for o in range(1, drafts):
                out = out + (decays[o - 1] * query_key[o]) * shift(delta, o)
            norm = lax.rsqrt(jnp.mean(out * out, axis=1, keepdims=True) + EPS)
            gate = gate_ref[:, vcols].astype(F32)
            mixed = (out * norm)[0:tok] * gain_ref[...] * jax.nn.silu(gate)
            if line:
                span = group * repeat * vwidth
                to = pl.multiple_of(step * span, span) + (repeat * i + j) * vwidth
                mixed_ref[0:tok, pl.ds(to, vwidth)] = mixed
            else:
                mixed_ref[:, vcols] = mixed.astype(BF16)
            written.append(column(1 + drafts) * delta)
            keeps.append(jnp.broadcast_to(column(2 + drafts), (pad, vwidth)))
        written = jnp.concatenate(written, axis=1)
        whigh = written.astype(BF16).astype(F32)
        wlow = written - whigh
        wrote = jnp.concatenate([whigh, wlow, whigh], axis=0).astype(BF16)
        kcat = jnp.concatenate([high[pad:], high[pad:], low[pad:]], axis=0)
        kspread = jnp.concatenate(
            [jnp.where(request3 == r, kcat, 0.0).astype(BF16) for r in range(reqs)], axis=1
        )
        update = lax.dot_general(
            kspread, wrote, (((0,), (0,)), ((), ())), preferred_element_type=F32
        )
        for r in range(reqs):
            for j in range(repeat):
                keep = keeps[j][r * drafts : r * drafts + 1, :]
                kept_ref[r, repeat * i + j] = (
                    keep * state_ref[r, repeat * i + j].astype(F32)
                    + update[r * width : (r + 1) * width, j * vwidth : (j + 1) * vwidth]
                ).astype(BF16)


    if not line:
        return

    @pl.when(step == pl.num_programs(0) - 1)
    def _():
        here = lax.axis_index("rows") // 4
        full = mixed_ref.shape[1]
        half, part = full // 2, full // line
        extra = pack.shape[1] - half
        pack[0:tok, 0:half] = mixed_ref[0:tok, 0:half]
        pack[tok : 2 * tok, 0:half] = mixed_ref[0:tok, half:full]
        for m in range(line):
            to = pl.multiple_of((here ^ m) * part, part)
            piece = residual_ref[:, pl.ds(to, part)].astype(F32)
            pack[0:tok, half : half + extra] = piece[:, 0:extra]
            pack[tok : 2 * tok, half : half + part - extra] = piece[:, extra:part]
            packed_refs[m][...] = pack[...].astype(BF16)


def delta_rule(
    query_in,
    key_in,
    value_in,
    gate_in,
    decay_in,
    beta_in,
    decay_rate,
    decay_bias,
    norm_gain,
    prior_state,
    accepted,
    line=0,
    residual=None,
    expert_ids=None,
    expert_scores=None,
):
    tok = query_in.shape[0]
    reqs, heads, width, vwidth = prior_state.shape
    drafts = tok // reqs
    query_heads = query_in.shape[1] // width
    repeat = heads // query_heads
    group = 2 if query_heads % 2 == 0 else 1
    pad = round_up(tok, 8)
    whole = lambda *shape: pl.BlockSpec(shape, lambda g: (0,) * len(shape))
    qblock = pl.BlockSpec((tok, group * width), lambda g: (0, g))
    vblock = pl.BlockSpec((tok, group * repeat * vwidth), lambda g: (0, g))
    sblock = pl.BlockSpec((reqs, group * repeat, width, vwidth), lambda g: (0, g, 0, 0))
    in_specs = [
        pl.BlockSpec(memory_space=pltpu.SMEM),
        qblock,
        qblock,
        vblock,
        vblock,
        whole(heads, tok),
        whole(heads, tok),
        whole(1, heads),
        whole(1, heads),
        whole(1, vwidth),
        sblock,
    ]
    args = [
        accepted,
        query_in,
        key_in,
        value_in,
        gate_in,
        decay_in.T,
        beta_in.T,
        decay_rate.reshape(1, heads),
        decay_bias.reshape(1, heads),
        norm_gain.reshape(1, vwidth),
        prior_state,
    ]
    scratch = [
        pltpu.VMEM((128, 128), F32),
        pltpu.VMEM((group, 2 * pad, width), F32),
        pltpu.VMEM((repeat, pad, vwidth), F32),
    ]
    kept = jax.ShapeDtypeStruct(prior_state.shape, BF16)
    full = heads * vwidth
    if line:
        packed = packed_shape(tok, full, line)
        out_specs = [whole(*packed)] * line + [sblock]
        out_shape = [jax.ShapeDtypeStruct(packed, BF16)] * line + [kept]
        scratch += [pltpu.VMEM((pad, full), F32), pltpu.VMEM(packed, F32)]
        top = expert_ids.shape[1]
        in_specs += [whole(tok, full), whole(top, tok), whole(top, tok)]
        args += [residual, expert_ids.T, expert_scores.T]
    else:
        out_specs = [vblock, sblock]
        out_shape = [jax.ShapeDtypeStruct((tok, full), BF16), kept]
    return pl.pallas_call(
        functools.partial(delta_kernel, drafts, group, line),
        grid=(query_heads // group,),
        in_specs=in_specs,
        out_specs=out_specs,
        out_shape=out_shape,
        scratch_shapes=scratch,
        compiler_params=pltpu.CompilerParams(vmem_limit_bytes=56 * 1024 * 1024),
        cost_estimate=pl.CostEstimate(
            flops=1024 * heads * reqs * width * vwidth * 16,
            bytes_accessed=64 * heads * reqs * width * vwidth,
            transcendentals=0,
        ),
    )(*args)


def packed_shape(tok, full, line):
    return (2 * tok, full // 2 + round_up(full // line + 128, 256) // 2)


def swap(values, mask):
    count = lax.axis_size("rows")
    return lax.ppermute(values, "rows", [(i, i ^ mask) for i in range(count)])


def run_experts(tokens, routes, ups, downs, numbers):
    total = None
    half = routes.shape[1] // 2
    for up, down, number in zip(ups, downs, numbers):
        inner = down.shape[0]
        full = jnp.dot(tokens, up, preferred_element_type=F32)
        here = lax.dynamic_slice(routes, (0, number), (routes.shape[0], 1)).astype(F32)
        rest = lax.dynamic_slice(routes, (0, half + number), (routes.shape[0], 1)).astype(F32)
        act = jax.nn.silu(full[:, :inner]) * full[:, inner:] * (here + rest)
        term = jnp.dot(act.astype(BF16), down, preferred_element_type=F32)
        total = term if total is None else total + term
    return total


def plane_layer(
    line,
    packed,
    out_weight,
    residual,
    post_gain,
    expert_up,
    expert_down,
):
    me = lax.axis_index("rows")
    here = me // 4
    tok, full = residual.shape
    exp_dev = expert_up.shape[0]
    part, half = full // line, full // 2
    extra = packed[0].shape[1] - half
    others = range(1, line)

    weight_x = swap(out_weight, 2)
    weight_core = swap(out_weight, 1)
    packed = list(packed)
    packed[-1], weight_x = lax.optimization_barrier((packed[-1], weight_x))
    weights = [out_weight, weight_core, weight_x, swap(weight_x, 1)]
    expert_up, expert_down, weights[3] = lax.optimization_barrier(
        (expert_up, expert_down, weights[3])
    )
    up_mate = swap(expert_up, 1)
    down_mate = swap(expert_down, 1)

    got = [packed[0]] + [swap(packed[m], 4 * m) for m in others]
    heads_in = [jnp.concatenate([g[:tok, :half], g[tok:, :half]], axis=1) for g in got]
    heads_in = jnp.concatenate(heads_in, axis=0)
    base = [
        jnp.concatenate([g[:tok, half:], g[tok:, half : half + part - extra]], axis=1) for g in got
    ]
    at = half + part - extra
    routes = jnp.concatenate([g[tok:, at : at + 128] for g in got], axis=0)
    attention = jnp.zeros((line * tok, part), F32)
    for mask, weight in enumerate(weights):
        piece = jnp.dot(heads_in, weight, preferred_element_type=F32)
        attention = lax.dynamic_update_slice(
            attention, piece, (0, ((me % 4) ^ mask) * piece.shape[1])
        )
    owner = jnp.arange(line * tok)[:, None] // tok
    base = jnp.concatenate(base, axis=0).astype(F32)
    columns = [(attention + jnp.where(owner == m, 0.0, base)).astype(BF16) for m in range(line)]

    hidden = jnp.zeros((line * tok, full), BF16)
    for m in range(line):
        piece = columns[m] if m == 0 else swap(columns[m], 4 * m)
        order = [piece[tok * (j ^ m) : tok * (j ^ m) + tok] for j in range(line)]
        hidden = lax.dynamic_update_slice(
            hidden, jnp.concatenate(order, axis=0), (0, (here ^ m) * part)
        )
    hidden = hidden.astype(F32)
    mine = hidden[:tok] + residual.astype(F32)
    hidden = jnp.concatenate([mine, hidden[tok:]], axis=0)
    scale = lax.rsqrt(jnp.mean(hidden * hidden, axis=1, keepdims=True) + EPS)
    normed = (hidden * scale * post_gain).astype(BF16)

    came = swap(jnp.concatenate([normed, routes], axis=1), 2)
    ups = [expert_up[i] for i in range(exp_dev)] + [up_mate[i] for i in range(exp_dev)]
    downs = [expert_down[i] for i in range(exp_dev)] + [down_mate[i] for i in range(exp_dev)]
    numbers = [who * exp_dev + i for who in (me, me ^ 1) for i in range(exp_dev)]
    own_sum = run_experts(normed, routes, ups, downs, numbers)
    far_sum = run_experts(came[:, :full], came[:, full:], ups, downs, numbers)
    total = own_sum + swap(far_sum.astype(BF16), 2).astype(F32)
    folded = []
    for m in range(line):
        rows = total[m * tok : (m + 1) * tok]
        folded.append(jnp.concatenate([rows[:, :half], rows[:, half:]], axis=0))
    out = folded[0]
    for m in others:
        out = out + swap(folded[m].astype(BF16), 4 * m).astype(F32)
    out = mine + jnp.concatenate([out[:tok], out[tok:]], axis=1)
    return out.astype(BF16)


def general_layer(
    mixed,
    out_weight,
    residual,
    post_gain,
    expert_ids,
    expert_scores,
    expert_up,
    expert_down,
):
    partial_value = jnp.dot(
        mixed,
        lax.all_gather(out_weight, "rows", axis=1, tiled=True),
        preferred_element_type=F32,
    )
    attention = lax.psum_scatter(partial_value, "heads", scatter_dimension=1, tiled=True)
    hidden_sum = residual.astype(F32) + attention
    full_width = residual.shape[1] * lax.axis_size("heads")
    square = lax.psum(jnp.sum(hidden_sum * hidden_sum, axis=1), "heads")
    inv_rms = lax.rsqrt(square / full_width + EPS)
    normed = (hidden_sum * inv_rms[:, None] * post_gain).astype(BF16)
    tok_rows, top_count = expert_ids.shape
    row_count = lax.axis_size("rows")
    exp_dev = expert_up.shape[0]
    experts_all = exp_dev * row_count
    capacity = max(2, (tok_rows * top_count + experts_all - 1) // experts_all + 1)
    half_width = normed.shape[1]
    flat_ids = expert_ids.reshape(-1)
    onehot = (flat_ids[:, None] == jnp.arange(experts_all, dtype=jnp.int32)[None, :]).astype(
        jnp.int32
    )
    earlier = jnp.cumsum(onehot, axis=0) - onehot
    slot_index = jnp.sum(earlier * onehot, axis=1)
    position = (flat_ids % exp_dev * row_count + flat_ids // exp_dev) * capacity + slot_index
    select = (
        jnp.arange(experts_all * capacity, dtype=jnp.int32)[:, None] == position[None, :]
    ).astype(BF16)
    spread = jnp.repeat(normed, top_count, axis=0)
    outgoing = jnp.dot(select, spread, preferred_element_type=F32).astype(BF16)
    outgoing = outgoing.reshape(exp_dev, row_count, capacity, half_width)
    arrived = lax.all_to_all(outgoing, "rows", split_axis=1, concat_axis=1, tiled=True)
    rows_in = arrived.reshape(exp_dev, row_count * capacity, half_width)
    partial_up = jnp.einsum("lnd,ldf->lnf", rows_in, expert_up, preferred_element_type=F32)
    full_up = lax.psum(partial_up, "heads")
    inner_width = expert_down.shape[1]
    activation = (jax.nn.silu(full_up[..., :inner_width]) * full_up[..., inner_width:]).astype(BF16)
    result = jnp.einsum("lnf,lfd->lnd", activation, expert_down, preferred_element_type=F32)
    returned = lax.all_to_all(
        result.astype(BF16).reshape(exp_dev, row_count, capacity, half_width),
        "rows",
        split_axis=1,
        concat_axis=1,
        tiled=True,
    )
    values_back = jnp.dot(select.T, returned.reshape(-1, half_width), preferred_element_type=F32)
    values_back = values_back.reshape(tok_rows, top_count, half_width)
    weights = expert_scores / jnp.sum(expert_scores, axis=1, keepdims=True)
    return (hidden_sum + jnp.sum(weights[:, :, None] * values_back, axis=1)).astype(BF16)


def per_device(mesh_shape, *args):
    delta_args, layer_args = args[:11], args[11:]
    rows = mesh_shape["rows"]
    if mesh_shape["heads"] == 1 and rows in (8, 16):
        line = rows // 4
        out_weight, residual, post_gain, ids, scores, up, down = layer_args
        *packed, kept_state = delta_rule(*delta_args, line, residual, ids, scores)
        layer_out = plane_layer(line, packed, out_weight, residual, post_gain, up, down)
    else:
        mixed, kept_state = delta_rule(*delta_args)
        layer_out = general_layer(mixed, *layer_args)
    return (layer_out, kept_state)


def solution(mesh):
    return jax.shard_map(
        functools.partial(per_device, dict(mesh.shape)),
        mesh=mesh,
        in_specs=(
            P(("groups", "rows"), "heads"),
            P(("groups", "rows"), "heads"),
            P(("groups", "rows"), "heads"),
            P(("groups", "rows"), "heads"),
            P(("groups", "rows"), "heads"),
            P(("groups", "rows"), "heads"),
            P("heads"),
            P("heads"),
            P(),
            P(("groups", "rows"), "heads", None, None),
            P(("groups", "rows")),
            P("heads", "rows"),
            P(("groups", "rows"), "heads"),
            P("heads"),
            P(("groups", "rows"), None),
            P(("groups", "rows"), None),
            P("rows", "heads", None),
            P("rows", None, "heads"),
        ),
        out_specs=(P(("groups", "rows"), "heads"), P(("groups", "rows"), "heads", None, None)),
        check_vma=False,
    )
```

```python
import functools

import jax
import jax.numpy as jnp
from jax import lax
from jax.experimental import pallas as pl
from jax.experimental.pallas import tpu as pltpu
from jax.sharding import PartitionSpec as P

EPS = 1e-06
BF16 = jnp.bfloat16
F32 = jnp.float32


def round_up(value, step):
    return -(-value // step) * step


def delta_kernel(
    drafts,
    group,
    line,
    accepted_ref,
    query_ref,
    key_ref,
    value_ref,
    gate_ref,
    decay_ref,
    beta_ref,
    rate_ref,
    bias_ref,
    gain_ref,
    state_ref,
    *refs,
):
    if line:
        residual_ref, ids_ref, scores_ref = refs[:3]
        packed_refs, refs = refs[3 : 3 + line], refs[3 + line :]
        written_ref, coef, unit, vals, mixed_ref, pack = refs
    else:
        mixed_ref, written_ref, coef, unit, vals = refs
    step = pl.program_id(0)
    tok = query_ref.shape[0]
    pad = unit.shape[1] // 2
    reqs, _, width, vwidth = state_ref.shape
    repeat = state_ref.shape[1] // group
    heads = decay_ref.shape[0]

    def shift(values, by):
        return pltpu.roll(values, by % pad, 0) if by % pad else values

    def ahead_of(values, by):
        return pltpu.roll(values, by % 128, 1) if by % 128 else values

    @pl.when(step == 0)
    def _():
        unit[...] = jnp.zeros_like(unit)
        vals[...] = jnp.zeros_like(vals)
        coef[...] = jnp.zeros_like(coef)
        square = (heads, heads)
        eye = lax.broadcasted_iota(jnp.int32, square, 0) == lax.broadcasted_iota(jnp.int32, square, 1)
        rate = jnp.sum(jnp.where(eye, rate_ref[...], 0.0), axis=1, keepdims=True)
        bias = jnp.sum(jnp.where(eye, bias_ref[...], 0.0), axis=1, keepdims=True)
        coef[0:heads, 0:tok] = -rate * jax.nn.softplus(decay_ref[...] + bias)
        coef[heads : 2 * heads, 0:tok] = jax.nn.sigmoid(beta_ref[...])
        log_decay = coef[0:heads]
        at = lax.broadcasted_iota(jnp.int32, log_decay.shape, 1)
        draft = at % drafts
        left = jnp.zeros_like(at)
        for r in range(reqs):
            left = jnp.where(at // drafts == r, accepted_ref[r], left)
        left = left - 1 - draft
        sums = [jnp.zeros_like(log_decay)]
        for o in range(drafts):
            sums.append(sums[-1] + ahead_of(log_decay, o))
        total = sums[1]
        for s in range(1, drafts):
            total = jnp.where(draft == s, sums[s + 1], total)
        coef[0:heads] = jnp.exp(total)
        for o in range(1, drafts):
            coef[(1 + o) * heads : (2 + o) * heads] = jnp.where(draft >= o, jnp.exp(sums[o]), 0.0)
        ahead = jnp.zeros_like(log_decay)
        later = jnp.zeros_like(log_decay)
        for o in range(1, drafts):
            ahead = ahead + ahead_of(log_decay, -o)
            later = jnp.where(left == o, ahead, later)
        coef[(1 + drafts) * heads : (2 + drafts) * heads] = jnp.where(
            left >= 0, jnp.exp(later), 0.0
        )
        coef[(2 + drafts) * heads : (3 + drafts) * heads] = jnp.exp(total + later)
        coef[...] = coef[...].T
        if line:
            rows = pack.shape[0] // 2
            half = mixed_ref.shape[1] // 2
            scores = scores_ref[...]
            scores = scores / jnp.sum(scores, axis=0, keepdims=True)
            experts = 64
            number = lax.broadcasted_iota(jnp.int32, (experts, tok), 0)
            dense = jnp.zeros((experts, tok), F32)
            for k in range(ids_ref.shape[0]):
                dense = dense + jnp.where(number == ids_ref[k : k + 1, :], scores[k : k + 1], 0.0)
            high = dense.astype(BF16).astype(F32)
            routes = jnp.concatenate([high, dense - high], axis=0)
            routes = jnp.concatenate(
                [routes, jnp.zeros((2 * experts, 128 - tok), F32)], axis=1
            ).T
            pack[...] = jnp.zeros_like(pack)
            part = mixed_ref.shape[1] // line
            at = half + part - (pack.shape[1] - half)
            pack[rows : 2 * rows, at : at + 128] = routes[0:tok]

    lane = lax.broadcasted_iota(jnp.int32, (pad, coef.shape[1]), 1)
    row = lax.broadcasted_iota(jnp.int32, (2 * pad, width), 0)
    request = row % pad // drafts
    for i in range(group):
        cols = slice(i * width, (i + 1) * width)
        for slot, ref, factor in ((0, query_ref, width ** (-0.5)), (1, key_ref, 1.0)):
            raw = ref[:, cols].astype(F32)
            scale = lax.rsqrt(jnp.sum(raw * raw, axis=1, keepdims=True) + EPS) * factor
            unit[i, slot * pad : slot * pad + tok, :] = raw * scale
        both = unit[i]
        high = both.astype(BF16).astype(F32)
        low = both - high
        spread = []
        for r in range(reqs):
            part = request == r
            spread.append(
                jnp.concatenate(
                    [jnp.where(part, high, 0.0), jnp.where(part, low, 0.0)], axis=0
                ).astype(BF16)
            )
        spread = jnp.concatenate(spread, axis=1)
        prior = jnp.concatenate(
            [
                jnp.concatenate([state_ref[r, repeat * i + j] for j in range(repeat)], axis=1)
                for r in range(reqs)
            ],
            axis=0,
        )
        read = jnp.dot(spread, prior, preferred_element_type=F32)
        query_prior = read[0:pad] + read[2 * pad : 3 * pad]
        key_prior = read[pad : 2 * pad] + read[3 * pad : 4 * pad]
        query, key = both[0:pad], both[pad : 2 * pad]
        shifted = [shift(key, o) for o in range(drafts)]
        query_key = [jnp.sum(query * s, axis=1, keepdims=True) for s in shifted]
        key_key = [jnp.sum(key * s, axis=1, keepdims=True) for s in shifted]
        for j in range(repeat):
            head = (step * group + i) * repeat + j
            vcols = slice((repeat * i + j) * vwidth, (repeat * i + j + 1) * vwidth)
            at = slice(j * vwidth, (j + 1) * vwidth)

            def column(index):
                mine = jnp.where(lane == index * heads + head, coef[0:pad], 0.0)
                return jnp.sum(mine, axis=1, keepdims=True)

            through, rate = column(0), column(1)
            decays = [column(1 + o) for o in range(1, drafts)]
            vals[j, 0:tok, :] = value_ref[:, vcols].astype(F32)
            base = rate * (vals[j] - through * key_prior[:, at])
            mixes = [rate * decays[o - 1] * key_key[o] for o in range(1, drafts)]
            delta = base
            for _ in range(1, drafts):
                delta = base - sum(mixes[o - 1] * shift(delta, o) for o in range(1, drafts))
            out = through * query_prior[:, at] + query_key[0] * delta
            for o in range(1, drafts):
                out = out + (decays[o - 1] * query_key[o]) * shift(delta, o)
            norm = lax.rsqrt(jnp.mean(out * out, axis=1, keepdims=True) + EPS)
            gate = gate_ref[:, vcols].astype(F32)
            mixed = (out * norm)[0:tok] * gain_ref[...] * jax.nn.silu(gate)
            if line:
                span = group * repeat * vwidth
                to = pl.multiple_of(step * span, span) + (repeat * i + j) * vwidth
                mixed_ref[0:tok, pl.ds(to, vwidth)] = mixed
            else:
                mixed_ref[:, vcols] = mixed.astype(BF16)
            written_ref[:, vcols] = column(1 + drafts) * delta
    if not line:
        return

    @pl.when(step == pl.num_programs(0) - 1)
    def _():
        here = lax.axis_index("rows") // 4
        full = mixed_ref.shape[1]
        half, part = full // 2, full // line
        extra = pack.shape[1] - half
        pack[0:tok, 0:half] = mixed_ref[0:tok, 0:half]
        pack[tok : 2 * tok, 0:half] = mixed_ref[0:tok, half:full]
        for m in range(line):
            to = pl.multiple_of((here ^ m) * part, part)
            piece = residual_ref[:, pl.ds(to, part)].astype(F32)
            pack[0:tok, half : half + extra] = piece[:, 0:extra]
            pack[tok : 2 * tok, half : half + part - extra] = piece[:, extra:part]
            packed_refs[m][...] = pack[...].astype(BF16)


def kept_kernel(
    drafts, group, key_ref, written_ref, coef_ref, state_ref, kept_ref, unit
):
    step = pl.program_id(0)
    tok = key_ref.shape[0]
    pad = written_ref.shape[0]
    reqs, _, width, vwidth = state_ref.shape
    repeat = state_ref.shape[1] // group
    heads = pl.num_programs(0) * group * repeat

    @pl.when(step == 0)
    def _():
        unit[...] = jnp.zeros_like(unit)

    lane = lax.broadcasted_iota(jnp.int32, (pad, coef_ref.shape[1]), 1)
    request = lax.broadcasted_iota(jnp.int32, (3 * pad, width), 0) % pad // drafts
    for i in range(group):
        raw = key_ref[:, i * width : (i + 1) * width].astype(F32)
        unit[i, 0:tok, :] = raw * lax.rsqrt(jnp.sum(raw * raw, axis=1, keepdims=True) + EPS)
        key = unit[i]
        high = key.astype(BF16).astype(F32)
        key = jnp.concatenate([high, high, key - high], axis=0)
        spread = jnp.concatenate(
            [jnp.where(request == r, key, 0.0).astype(BF16) for r in range(reqs)], axis=1
        )
        written = written_ref[:, i * repeat * vwidth : (i + 1) * repeat * vwidth]
        high = written.astype(BF16).astype(F32)
        wrote = jnp.concatenate([high, written - high, high], axis=0).astype(BF16)
        update = lax.dot_general(
            spread, wrote, (((0,), (0,)), ((), ())), preferred_element_type=F32
        )
        for j in range(repeat):
            head = (step * group + i) * repeat + j
            mine = jnp.where(lane == (2 + drafts) * heads + head, coef_ref[0:pad], 0.0)
            keep = jnp.broadcast_to(jnp.sum(mine, axis=1, keepdims=True), (pad, vwidth))
            for r in range(reqs):
                kept_ref[r, repeat * i + j] = (
                    keep[r * drafts : r * drafts + 1, :] * state_ref[r, repeat * i + j].astype(F32)
                    + update[r * width : (r + 1) * width, j * vwidth : (j + 1) * vwidth]
                ).astype(BF16)


def delta_rule(
    query_in,
    key_in,
    value_in,
    gate_in,
    decay_in,
    beta_in,
    decay_rate,
    decay_bias,
    norm_gain,
    prior_state,
    accepted,
    line=0,
    residual=None,
    expert_ids=None,
    expert_scores=None,
):
    tok = query_in.shape[0]
    reqs, heads, width, vwidth = prior_state.shape
    drafts = tok // reqs
    query_heads = query_in.shape[1] // width
    repeat = heads // query_heads
    group = 4 if query_heads % 4 == 0 else 1
    pad = round_up(tok, 8)
    whole = lambda *shape: pl.BlockSpec(shape, lambda g: (0,) * len(shape))
    qblock = pl.BlockSpec((tok, group * width), lambda g: (0, g))
    vblock = pl.BlockSpec((tok, group * repeat * vwidth), lambda g: (0, g))
    sblock = pl.BlockSpec((reqs, group * repeat, width, vwidth), lambda g: (0, g, 0, 0))
    in_specs = [
        pl.BlockSpec(memory_space=pltpu.SMEM),
        qblock,
        qblock,
        vblock,
        vblock,
        whole(heads, tok),
        whole(heads, tok),
        whole(1, heads),
        whole(1, heads),
        whole(1, vwidth),
        sblock,
    ]
    args = [
        accepted,
        query_in,
        key_in,
        value_in,
        gate_in,
        decay_in.T,
        beta_in.T,
        decay_rate.reshape(1, heads),
        decay_bias.reshape(1, heads),
        norm_gain.reshape(1, vwidth),
        prior_state,
    ]
    scratch = [
        pltpu.VMEM((group, 2 * pad, width), F32),
        pltpu.VMEM((repeat, pad, vwidth), F32),
    ]
    full = heads * vwidth
    out_specs = [pl.BlockSpec((pad, group * repeat * vwidth), lambda g: (0, g)), whole(128, 128)]
    out_shape = [jax.ShapeDtypeStruct((pad, full), F32), jax.ShapeDtypeStruct((128, 128), F32)]
    if line:
        packed = packed_shape(tok, full, line)
        out_specs = [whole(*packed)] * line + out_specs
        out_shape = [jax.ShapeDtypeStruct(packed, BF16)] * line + out_shape
        scratch += [pltpu.VMEM((pad, full), F32), pltpu.VMEM(packed, F32)]
        top = expert_ids.shape[1]
        in_specs += [whole(tok, full), whole(top, tok), whole(top, tok)]
        args += [residual, expert_ids.T, expert_scores.T]
    else:
        out_specs = [vblock] + out_specs
        out_shape = [jax.ShapeDtypeStruct((tok, full), BF16)] + out_shape
    cells = heads * reqs * width * vwidth
    grid = (query_heads // group,)
    *mixed, written, coef = pl.pallas_call(
        functools.partial(delta_kernel, drafts, group, line),
        grid=grid,
        in_specs=in_specs,
        out_specs=out_specs,
        out_shape=out_shape,
        scratch_shapes=scratch,
        compiler_params=pltpu.CompilerParams(vmem_limit_bytes=56 * 1024 * 1024),
        cost_estimate=pl.CostEstimate(
            flops=8192 * cells, bytes_accessed=64 * cells, transcendentals=0
        ),
    )(*args)
    kept = pl.pallas_call(
        functools.partial(kept_kernel, drafts, group),
        grid=grid,
        in_specs=[
            qblock,
            pl.BlockSpec((pad, group * repeat * vwidth), lambda g: (0, g)),
            whole(128, 128),
            sblock,
        ],
        out_specs=sblock,
        out_shape=jax.ShapeDtypeStruct(prior_state.shape, BF16),
        scratch_shapes=[pltpu.VMEM((group, pad, width), F32)],
        compiler_params=pltpu.CompilerParams(vmem_limit_bytes=56 * 1024 * 1024),
        cost_estimate=pl.CostEstimate(
            flops=8192 * cells, bytes_accessed=64 * cells, transcendentals=0
        ),
    )(key_in, written, coef, prior_state)
    return (*mixed, kept)


def packed_shape(tok, full, line):
    return (2 * tok, full // 2 + round_up(full // line + 128, 256) // 2)


def swap(values, mask):
    count = lax.axis_size("rows")
    return lax.ppermute(values, "rows", [(i, i ^ mask) for i in range(count)])


def run_experts(tokens, routes, ups, downs, numbers):
    total = None
    half = routes.shape[1] // 2
    for up, down, number in zip(ups, downs, numbers):
        inner = down.shape[0]
        full = jnp.dot(tokens, up, preferred_element_type=F32)
        here = lax.dynamic_slice(routes, (0, number), (routes.shape[0], 1)).astype(F32)
        rest = lax.dynamic_slice(routes, (0, half + number), (routes.shape[0], 1)).astype(F32)
        act = jax.nn.silu(full[:, :inner]) * full[:, inner:] * (here + rest)
        term = jnp.dot(act.astype(BF16), down, preferred_element_type=F32)
        total = term if total is None else total + term
    return total


def plane_layer(
    line,
    packed,
    out_weight,
    residual,
    post_gain,
    expert_up,
    expert_down,
):
    me = lax.axis_index("rows")
    here = me // 4
    tok, full = residual.shape
    exp_dev = expert_up.shape[0]
    part, half = full // line, full // 2
    extra = packed[0].shape[1] - half
    others = range(1, line)

    weight_x = swap(out_weight, 2)
    weight_core = swap(out_weight, 1)

    got = [packed[0]] + [swap(packed[m], 4 * m) for m in others]
    got[1], weight_x = lax.optimization_barrier((got[1], weight_x))
    weights = [out_weight, weight_core, weight_x, swap(weight_x, 1)]
    expert_up, expert_down, weights[3] = lax.optimization_barrier(
        (expert_up, expert_down, weights[3])
    )
    up_mate = swap(expert_up, 1)
    down_mate = swap(expert_down, 1)
    heads_in = [jnp.concatenate([g[:tok, :half], g[tok:, :half]], axis=1) for g in got]
    heads_in = jnp.concatenate(heads_in, axis=0)
    base = [
        jnp.concatenate([g[:tok, half:], g[tok:, half : half + part - extra]], axis=1) for g in got
    ]
    at = half + part - extra
    routes = jnp.concatenate([g[tok:, at : at + 128] for g in got], axis=0)
    attention = jnp.zeros((line * tok, part), F32)
    for mask, weight in enumerate(weights):
        piece = jnp.dot(heads_in, weight, preferred_element_type=F32)
        attention = lax.dynamic_update_slice(
            attention, piece, (0, ((me % 4) ^ mask) * piece.shape[1])
        )
    owner = jnp.arange(line * tok)[:, None] // tok
    base = jnp.concatenate(base, axis=0).astype(F32)
    columns = [(attention + jnp.where(owner == m, 0.0, base)).astype(BF16) for m in range(line)]

    hidden = jnp.zeros((line * tok, full), BF16)
    for m in range(line):
        piece = columns[m] if m == 0 else swap(columns[m], 4 * m)
        order = [piece[tok * (j ^ m) : tok * (j ^ m) + tok] for j in range(line)]
        hidden = lax.dynamic_update_slice(
            hidden, jnp.concatenate(order, axis=0), (0, (here ^ m) * part)
        )
    hidden = hidden.astype(F32)
    mine = hidden[:tok] + residual.astype(F32)
    hidden = jnp.concatenate([mine, hidden[tok:]], axis=0)
    scale = lax.rsqrt(jnp.mean(hidden * hidden, axis=1, keepdims=True) + EPS)
    normed = (hidden * scale * post_gain).astype(BF16)

    came = swap(jnp.concatenate([normed, routes], axis=1), 2)
    ups = [expert_up[i] for i in range(exp_dev)] + [up_mate[i] for i in range(exp_dev)]
    downs = [expert_down[i] for i in range(exp_dev)] + [down_mate[i] for i in range(exp_dev)]
    numbers = [who * exp_dev + i for who in (me, me ^ 1) for i in range(exp_dev)]
    own_sum = run_experts(normed, routes, ups, downs, numbers)
    far_sum = run_experts(came[:, :full], came[:, full:], ups, downs, numbers)
    total = own_sum + swap(far_sum.astype(BF16), 2).astype(F32)
    folded = []
    for m in range(line):
        rows = total[m * tok : (m + 1) * tok]
        folded.append(jnp.concatenate([rows[:, :half], rows[:, half:]], axis=0))
    out = folded[0]
    for m in others:
        out = out + swap(folded[m].astype(BF16), 4 * m).astype(F32)
    out = mine + jnp.concatenate([out[:tok], out[tok:]], axis=1)
    return out.astype(BF16)


def general_layer(
    mixed,
    out_weight,
    residual,
    post_gain,
    expert_ids,
    expert_scores,
    expert_up,
    expert_down,
):
    partial_value = jnp.dot(
        mixed,
        lax.all_gather(out_weight, "rows", axis=1, tiled=True),
        preferred_element_type=F32,
    )
    attention = lax.psum_scatter(partial_value, "heads", scatter_dimension=1, tiled=True)
    hidden_sum = residual.astype(F32) + attention
    full_width = residual.shape[1] * lax.axis_size("heads")
    square = lax.psum(jnp.sum(hidden_sum * hidden_sum, axis=1), "heads")
    inv_rms = lax.rsqrt(square / full_width + EPS)
    normed = (hidden_sum * inv_rms[:, None] * post_gain).astype(BF16)
    tok_rows, top_count = expert_ids.shape
    row_count = lax.axis_size("rows")
    exp_dev = expert_up.shape[0]
    experts_all = exp_dev * row_count
    capacity = max(2, (tok_rows * top_count + experts_all - 1) // experts_all + 1)
    half_width = normed.shape[1]
    flat_ids = expert_ids.reshape(-1)
    onehot = (flat_ids[:, None] == jnp.arange(experts_all, dtype=jnp.int32)[None, :]).astype(
        jnp.int32
    )
    earlier = jnp.cumsum(onehot, axis=0) - onehot
    slot_index = jnp.sum(earlier * onehot, axis=1)
    position = (flat_ids % exp_dev * row_count + flat_ids // exp_dev) * capacity + slot_index
    select = (
        jnp.arange(experts_all * capacity, dtype=jnp.int32)[:, None] == position[None, :]
    ).astype(BF16)
    spread = jnp.repeat(normed, top_count, axis=0)
    outgoing = jnp.dot(select, spread, preferred_element_type=F32).astype(BF16)
    outgoing = outgoing.reshape(exp_dev, row_count, capacity, half_width)
    arrived = lax.all_to_all(outgoing, "rows", split_axis=1, concat_axis=1, tiled=True)
    rows_in = arrived.reshape(exp_dev, row_count * capacity, half_width)
    partial_up = jnp.einsum("lnd,ldf->lnf", rows_in, expert_up, preferred_element_type=F32)
    full_up = lax.psum(partial_up, "heads")
    inner_width = expert_down.shape[1]
    activation = (jax.nn.silu(full_up[..., :inner_width]) * full_up[..., inner_width:]).astype(BF16)
    result = jnp.einsum("lnf,lfd->lnd", activation, expert_down, preferred_element_type=F32)
    returned = lax.all_to_all(
        result.astype(BF16).reshape(exp_dev, row_count, capacity, half_width),
        "rows",
        split_axis=1,
        concat_axis=1,
        tiled=True,
    )
    values_back = jnp.dot(select.T, returned.reshape(-1, half_width), preferred_element_type=F32)
    values_back = values_back.reshape(tok_rows, top_count, half_width)
    weights = expert_scores / jnp.sum(expert_scores, axis=1, keepdims=True)
    return (hidden_sum + jnp.sum(weights[:, :, None] * values_back, axis=1)).astype(BF16)


def per_device(mesh_shape, *args):
    delta_args, layer_args = args[:11], args[11:]
    rows = mesh_shape["rows"]
    if mesh_shape["heads"] == 1 and rows in (8, 16):
        line = rows // 4
        out_weight, residual, post_gain, ids, scores, up, down = layer_args
        *packed, kept_state = delta_rule(*delta_args, line, residual, ids, scores)
        layer_out = plane_layer(line, packed, out_weight, residual, post_gain, up, down)
    else:
        mixed, kept_state = delta_rule(*delta_args)
        layer_out = general_layer(mixed, *layer_args)
    return (layer_out, kept_state)


def solution(mesh):
    return jax.shard_map(
        functools.partial(per_device, dict(mesh.shape)),
        mesh=mesh,
        in_specs=(
            P(("groups", "rows"), "heads"),
            P(("groups", "rows"), "heads"),
            P(("groups", "rows"), "heads"),
            P(("groups", "rows"), "heads"),
            P(("groups", "rows"), "heads"),
            P(("groups", "rows"), "heads"),
            P("heads"),
            P("heads"),
            P(),
            P(("groups", "rows"), "heads", None, None),
            P(("groups", "rows")),
            P("heads", "rows"),
            P(("groups", "rows"), "heads"),
            P("heads"),
            P(("groups", "rows"), None),
            P(("groups", "rows"), None),
            P("rows", "heads", None),
            P("rows", None, "heads"),
        ),
        out_specs=(P(("groups", "rows"), "heads"), P(("groups", "rows"), "heads", None, None)),
        check_vma=False,
    )
```

```python
import functools

import jax
import jax.numpy as jnp
from jax import lax
from jax.experimental import pallas as pl
from jax.experimental.pallas import tpu as pltpu
from jax.sharding import PartitionSpec as P

EPS = 1e-06
BF16 = jnp.bfloat16
F32 = jnp.float32


def round_up(value, step):
    return -(-value // step) * step


def delta_kernel(
    drafts,
    group,
    line,
    accepted_ref,
    query_ref,
    key_ref,
    value_ref,
    gate_ref,
    decay_ref,
    beta_ref,
    rate_ref,
    bias_ref,
    gain_ref,
    state_ref,
    *refs,
):
    if line:
        residual_ref, ids_ref, scores_ref = refs[:3]
        packed_refs, refs = refs[3 : 3 + line], refs[3 + line :]
        written_ref, coef, unit, vals, mixed_ref, pack = refs
    else:
        mixed_ref, written_ref, coef, unit, vals = refs
    step = pl.program_id(0)
    tok = query_ref.shape[0]
    pad = unit.shape[1] // 2
    reqs, _, width, vwidth = state_ref.shape
    repeat = state_ref.shape[1] // group
    heads = decay_ref.shape[0]

    def shift(values, by):
        return pltpu.roll(values, by % pad, 0) if by % pad else values

    def ahead_of(values, by):
        return pltpu.roll(values, by % 128, 1) if by % 128 else values

    @pl.when(step == 0)
    def _():
        unit[...] = jnp.zeros_like(unit)
        vals[...] = jnp.zeros_like(vals)
        coef[...] = jnp.zeros_like(coef)
        square = (heads, heads)
        eye = lax.broadcasted_iota(jnp.int32, square, 0) == lax.broadcasted_iota(jnp.int32, square, 1)
        rate = jnp.sum(jnp.where(eye, rate_ref[...], 0.0), axis=1, keepdims=True)
        bias = jnp.sum(jnp.where(eye, bias_ref[...], 0.0), axis=1, keepdims=True)
        coef[0:heads, 0:tok] = -rate * jax.nn.softplus(decay_ref[...] + bias)
        coef[heads : 2 * heads, 0:tok] = jax.nn.sigmoid(beta_ref[...])
        log_decay = coef[0:heads]
        at = lax.broadcasted_iota(jnp.int32, log_decay.shape, 1)
        draft = at % drafts
        left = jnp.zeros_like(at)
        for r in range(reqs):
            left = jnp.where(at // drafts == r, accepted_ref[r], left)
        left = left - 1 - draft
        sums = [jnp.zeros_like(log_decay)]
        for o in range(drafts):
            sums.append(sums[-1] + ahead_of(log_decay, o))
        total = sums[1]
        for s in range(1, drafts):
            total = jnp.where(draft == s, sums[s + 1], total)
        coef[0:heads] = jnp.exp(total)
        for o in range(1, drafts):
            coef[(1 + o) * heads : (2 + o) * heads] = jnp.where(draft >= o, jnp.exp(sums[o]), 0.0)
        ahead = jnp.zeros_like(log_decay)
        later = jnp.zeros_like(log_decay)
        for o in range(1, drafts):
            ahead = ahead + ahead_of(log_decay, -o)
            later = jnp.where(left == o, ahead, later)
        coef[(1 + drafts) * heads : (2 + drafts) * heads] = jnp.where(
            left >= 0, jnp.exp(later), 0.0
        )
        coef[(2 + drafts) * heads : (3 + drafts) * heads] = jnp.exp(total + later)
        coef[...] = coef[...].T
        if line:
            rows = pack.shape[0] // 2
            half = mixed_ref.shape[1] // 2
            scores = scores_ref[...]
            scores = scores / jnp.sum(scores, axis=0, keepdims=True)
            experts = 64
            number = lax.broadcasted_iota(jnp.int32, (experts, tok), 0)
            dense = jnp.zeros((experts, tok), F32)
            for k in range(ids_ref.shape[0]):
                dense = dense + jnp.where(number == ids_ref[k : k + 1, :], scores[k : k + 1], 0.0)
            high = dense.astype(BF16).astype(F32)
            routes = jnp.concatenate([high, dense - high], axis=0)
            routes = jnp.concatenate(
                [routes, jnp.zeros((2 * experts, 128 - tok), F32)], axis=1
            ).T
            pack[...] = jnp.zeros_like(pack)
            part = mixed_ref.shape[1] // line
            at = half + part - (pack.shape[1] - half)
            pack[rows : 2 * rows, at : at + 128] = routes[0:tok]

    lane = lax.broadcasted_iota(jnp.int32, (pad, coef.shape[1]), 1)
    row = lax.broadcasted_iota(jnp.int32, (2 * pad, width), 0)
    request = row % pad // drafts
    for i in range(group):
        cols = slice(i * width, (i + 1) * width)
        for slot, ref, factor in ((0, query_ref, width ** (-0.5)), (1, key_ref, 1.0)):
            raw = ref[:, cols].astype(F32)
            scale = lax.rsqrt(jnp.sum(raw * raw, axis=1, keepdims=True) + EPS) * factor
            unit[i, slot * pad : slot * pad + tok, :] = raw * scale
        both = unit[i]
        high = both.astype(BF16).astype(F32)
        low = both - high
        spread = []
        for r in range(reqs):
            part = request == r
            spread.append(
                jnp.concatenate(
                    [jnp.where(part, high, 0.0), jnp.where(part, low, 0.0)], axis=0
                ).astype(BF16)
            )
        spread = jnp.concatenate(spread, axis=1)
        prior = jnp.concatenate(
            [
                jnp.concatenate([state_ref[r, repeat * i + j] for j in range(repeat)], axis=1)
                for r in range(reqs)
            ],
            axis=0,
        )
        read = jnp.dot(spread, prior, preferred_element_type=F32)
        query_prior = read[0:pad] + read[2 * pad : 3 * pad]
        key_prior = read[pad : 2 * pad] + read[3 * pad : 4 * pad]
        query, key = both[0:pad], both[pad : 2 * pad]
        shifted = [shift(key, o) for o in range(drafts)]
        query_key = [jnp.sum(query * s, axis=1, keepdims=True) for s in shifted]
        key_key = [jnp.sum(key * s, axis=1, keepdims=True) for s in shifted]
        for j in range(repeat):
            head = (step * group + i) * repeat + j
            vcols = slice((repeat * i + j) * vwidth, (repeat * i + j + 1) * vwidth)
            at = slice(j * vwidth, (j + 1) * vwidth)

            def column(index):
                mine = jnp.where(lane == index * heads + head, coef[0:pad], 0.0)
                return jnp.sum(mine, axis=1, keepdims=True)

            through, rate = column(0), column(1)
            decays = [column(1 + o) for o in range(1, drafts)]
            vals[j, 0:tok, :] = value_ref[:, vcols].astype(F32)
            base = rate * (vals[j] - through * key_prior[:, at])
            mixes = [rate * decays[o - 1] * key_key[o] for o in range(1, drafts)]
            delta = base
            for _ in range(1, drafts):
                delta = base - sum(mixes[o - 1] * shift(delta, o) for o in range(1, drafts))
            out = through * query_prior[:, at] + query_key[0] * delta
            for o in range(1, drafts):
                out = out + (decays[o - 1] * query_key[o]) * shift(delta, o)
            norm = lax.rsqrt(jnp.mean(out * out, axis=1, keepdims=True) + EPS)
            gate = gate_ref[:, vcols].astype(F32)
            mixed = (out * norm)[0:tok] * gain_ref[...] * jax.nn.silu(gate)
            if line:
                span = group * repeat * vwidth
                to = pl.multiple_of(step * span, span) + (repeat * i + j) * vwidth
                mixed_ref[0:tok, pl.ds(to, vwidth)] = mixed
            else:
                mixed_ref[:, vcols] = mixed.astype(BF16)
            written_ref[:, vcols] = column(1 + drafts) * delta
    if not line:
        return

    @pl.when(step == pl.num_programs(0) - 1)
    def _():
        here = lax.axis_index("rows") // 4
        full = mixed_ref.shape[1]
        half, part = full // 2, full // line
        extra = pack.shape[1] - half
        pack[0:tok, 0:half] = mixed_ref[0:tok, 0:half]
        pack[tok : 2 * tok, 0:half] = mixed_ref[0:tok, half:full]
        for m in range(line):
            to = pl.multiple_of((here ^ m) * part, part)
            piece = residual_ref[:, pl.ds(to, part)].astype(F32)
            pack[0:tok, half : half + extra] = piece[:, 0:extra]
            pack[tok : 2 * tok, half : half + part - extra] = piece[:, extra:part]
            packed_refs[m][...] = pack[...].astype(BF16)


def kept_kernel(
    drafts, group, key_ref, written_ref, coef_ref, state_ref, kept_ref, unit
):
    step = pl.program_id(0)
    tok = key_ref.shape[0]
    pad = written_ref.shape[0]
    reqs, _, width, vwidth = state_ref.shape
    repeat = state_ref.shape[1] // group
    heads = pl.num_programs(0) * group * repeat

    @pl.when(step == 0)
    def _():
        unit[...] = jnp.zeros_like(unit)

    lane = lax.broadcasted_iota(jnp.int32, (pad, coef_ref.shape[1]), 1)
    request = lax.broadcasted_iota(jnp.int32, (3 * pad, width), 0) % pad // drafts
    for i in range(group):
        raw = key_ref[:, i * width : (i + 1) * width].astype(F32)
        unit[i, 0:tok, :] = raw * lax.rsqrt(jnp.sum(raw * raw, axis=1, keepdims=True) + EPS)
        key = unit[i]
        high = key.astype(BF16).astype(F32)
        key = jnp.concatenate([high, high, key - high], axis=0)
        spread = jnp.concatenate(
            [jnp.where(request == r, key, 0.0).astype(BF16) for r in range(reqs)], axis=1
        )
        written = written_ref[:, i * repeat * vwidth : (i + 1) * repeat * vwidth]
        high = written.astype(BF16).astype(F32)
        wrote = jnp.concatenate([high, written - high, high], axis=0).astype(BF16)
        update = lax.dot_general(
            spread, wrote, (((0,), (0,)), ((), ())), preferred_element_type=F32
        )
        for j in range(repeat):
            head = (step * group + i) * repeat + j
            mine = jnp.where(lane == (2 + drafts) * heads + head, coef_ref[0:pad], 0.0)
            keep = jnp.broadcast_to(jnp.sum(mine, axis=1, keepdims=True), (pad, vwidth))
            for r in range(reqs):
                kept_ref[r, repeat * i + j] = (
                    keep[r * drafts : r * drafts + 1, :] * state_ref[r, repeat * i + j].astype(F32)
                    + update[r * width : (r + 1) * width, j * vwidth : (j + 1) * vwidth]
                ).astype(BF16)


def delta_rule(
    query_in,
    key_in,
    value_in,
    gate_in,
    decay_in,
    beta_in,
    decay_rate,
    decay_bias,
    norm_gain,
    prior_state,
    accepted,
    line=0,
    residual=None,
    expert_ids=None,
    expert_scores=None,
):
    tok = query_in.shape[0]
    reqs, heads, width, vwidth = prior_state.shape
    drafts = tok // reqs
    query_heads = query_in.shape[1] // width
    repeat = heads // query_heads
    group = 4 if query_heads % 4 == 0 else 1
    pad = round_up(tok, 8)
    whole = lambda *shape: pl.BlockSpec(shape, lambda g: (0,) * len(shape))
    qblock = pl.BlockSpec((tok, group * width), lambda g: (0, g))
    vblock = pl.BlockSpec((tok, group * repeat * vwidth), lambda g: (0, g))
    sblock = pl.BlockSpec((reqs, group * repeat, width, vwidth), lambda g: (0, g, 0, 0))
    in_specs = [
        pl.BlockSpec(memory_space=pltpu.SMEM),
        qblock,
        qblock,
        vblock,
        vblock,
        whole(heads, tok),
        whole(heads, tok),
        whole(1, heads),
        whole(1, heads),
        whole(1, vwidth),
        sblock,
    ]
    args = [
        accepted,
        query_in,
        key_in,
        value_in,
        gate_in,
        decay_in.T,
        beta_in.T,
        decay_rate.reshape(1, heads),
        decay_bias.reshape(1, heads),
        norm_gain.reshape(1, vwidth),
        prior_state,
    ]
    scratch = [
        pltpu.VMEM((group, 2 * pad, width), F32),
        pltpu.VMEM((repeat, pad, vwidth), F32),
    ]
    full = heads * vwidth
    out_specs = [pl.BlockSpec((pad, group * repeat * vwidth), lambda g: (0, g)), whole(128, 128)]
    out_shape = [jax.ShapeDtypeStruct((pad, full), F32), jax.ShapeDtypeStruct((128, 128), F32)]
    if line:
        packed = packed_shape(tok, full, line)
        out_specs = [whole(*packed)] * line + out_specs
        out_shape = [jax.ShapeDtypeStruct(packed, BF16)] * line + out_shape
        scratch += [pltpu.VMEM((pad, full), F32), pltpu.VMEM(packed, F32)]
        top = expert_ids.shape[1]
        in_specs += [whole(tok, full), whole(top, tok), whole(top, tok)]
        args += [residual, expert_ids.T, expert_scores.T]
    else:
        out_specs = [vblock] + out_specs
        out_shape = [jax.ShapeDtypeStruct((tok, full), BF16)] + out_shape
    cells = heads * reqs * width * vwidth
    grid = (query_heads // group,)
    *mixed, written, coef = pl.pallas_call(
        functools.partial(delta_kernel, drafts, group, line),
        grid=grid,
        in_specs=in_specs,
        out_specs=out_specs,
        out_shape=out_shape,
        scratch_shapes=scratch,
        compiler_params=pltpu.CompilerParams(vmem_limit_bytes=56 * 1024 * 1024),
        cost_estimate=pl.CostEstimate(
            flops=512 * cells, bytes_accessed=4 * cells, transcendentals=0
        ),
    )(*args)
    kept = pl.pallas_call(
        functools.partial(kept_kernel, drafts, group),
        grid=grid,
        in_specs=[
            qblock,
            pl.BlockSpec((pad, group * repeat * vwidth), lambda g: (0, g)),
            whole(128, 128),
            sblock,
        ],
        out_specs=sblock,
        out_shape=jax.ShapeDtypeStruct(prior_state.shape, BF16),
        scratch_shapes=[pltpu.VMEM((group, pad, width), F32)],
        compiler_params=pltpu.CompilerParams(vmem_limit_bytes=56 * 1024 * 1024),
        cost_estimate=pl.CostEstimate(
            flops=512 * cells, bytes_accessed=4 * cells, transcendentals=0
        ),
    )(key_in, written, coef, prior_state)
    return (*mixed, kept)


def packed_shape(tok, full, line):
    return (2 * tok, full // 2 + round_up(full // line + 128, 256) // 2)


def swap(values, mask):
    count = lax.axis_size("rows")
    return lax.ppermute(values, "rows", [(i, i ^ mask) for i in range(count)])


def run_experts(tokens, routes, ups, downs, numbers):
    total = None
    half = routes.shape[1] // 2
    for up, down, number in zip(ups, downs, numbers):
        inner = down.shape[0]
        full = jnp.dot(tokens, up, preferred_element_type=F32)
        here = lax.dynamic_slice(routes, (0, number), (routes.shape[0], 1)).astype(F32)
        rest = lax.dynamic_slice(routes, (0, half + number), (routes.shape[0], 1)).astype(F32)
        act = jax.nn.silu(full[:, :inner]) * full[:, inner:] * (here + rest)
        term = jnp.dot(act.astype(BF16), down, preferred_element_type=F32)
        total = term if total is None else total + term
    return total


def plane_layer(
    line,
    packed,
    out_weight,
    residual,
    post_gain,
    expert_up,
    expert_down,
):
    me = lax.axis_index("rows")
    here = me // 4
    tok, full = residual.shape
    exp_dev = expert_up.shape[0]
    part, half = full // line, full // 2
    extra = packed[0].shape[1] - half
    others = range(1, line)

    weight_x = swap(out_weight, 2)
    weight_core = swap(out_weight, 1)

    got = [packed[0]] + [swap(packed[m], 4 * m) for m in others]
    got[1], weight_x = lax.optimization_barrier((got[1], weight_x))
    weights = [out_weight, weight_core, weight_x, swap(weight_x, 1)]
    expert_up, expert_down, weights[3] = lax.optimization_barrier(
        (expert_up, expert_down, weights[3])
    )
    up_mate = swap(expert_up, 1)
    down_mate = swap(expert_down, 1)
    heads_in = [jnp.concatenate([g[:tok, :half], g[tok:, :half]], axis=1) for g in got]
    heads_in = jnp.concatenate(heads_in, axis=0)
    base = [
        jnp.concatenate([g[:tok, half:], g[tok:, half : half + part - extra]], axis=1) for g in got
    ]
    at = half + part - extra
    routes = jnp.concatenate([g[tok:, at : at + 128] for g in got], axis=0)
    attention = jnp.zeros((line * tok, part), F32)
    for mask, weight in enumerate(weights):
        piece = jnp.dot(heads_in, weight, preferred_element_type=F32)
        attention = lax.dynamic_update_slice(
            attention, piece, (0, ((me % 4) ^ mask) * piece.shape[1])
        )
    owner = jnp.arange(line * tok)[:, None] // tok
    base = jnp.concatenate(base, axis=0).astype(F32)
    columns = [(attention + jnp.where(owner == m, 0.0, base)).astype(BF16) for m in range(line)]

    hidden = jnp.zeros((line * tok, full), BF16)
    for m in range(line):
        piece = columns[m] if m == 0 else swap(columns[m], 4 * m)
        order = [piece[tok * (j ^ m) : tok * (j ^ m) + tok] for j in range(line)]
        hidden = lax.dynamic_update_slice(
            hidden, jnp.concatenate(order, axis=0), (0, (here ^ m) * part)
        )
    hidden = hidden.astype(F32)
    mine = hidden[:tok] + residual.astype(F32)
    hidden = jnp.concatenate([mine, hidden[tok:]], axis=0)
    scale = lax.rsqrt(jnp.mean(hidden * hidden, axis=1, keepdims=True) + EPS)
    normed = (hidden * scale * post_gain).astype(BF16)

    came = swap(normed, 2)
    far_routes = swap(routes, 2)
    ups = [expert_up[i] for i in range(exp_dev)] + [up_mate[i] for i in range(exp_dev)]
    downs = [expert_down[i] for i in range(exp_dev)] + [down_mate[i] for i in range(exp_dev)]
    numbers = [who * exp_dev + i for who in (me, me ^ 1) for i in range(exp_dev)]
    own_sum = run_experts(normed, routes, ups, downs, numbers)
    far_sum = run_experts(came, far_routes, ups, downs, numbers)
    total = own_sum + swap(far_sum.astype(BF16), 2).astype(F32)
    folded = []
    for m in range(line):
        rows = total[m * tok : (m + 1) * tok]
        folded.append(jnp.concatenate([rows[:, :half], rows[:, half:]], axis=0))
    out = folded[0]
    for m in others:
        out = out + swap(folded[m].astype(BF16), 4 * m).astype(F32)
    out = mine + jnp.concatenate([out[:tok], out[tok:]], axis=1)
    return out.astype(BF16)


def general_layer(
    mixed,
    out_weight,
    residual,
    post_gain,
    expert_ids,
    expert_scores,
    expert_up,
    expert_down,
):
    partial_value = jnp.dot(
        mixed,
        lax.all_gather(out_weight, "rows", axis=1, tiled=True),
        preferred_element_type=F32,
    )
    attention = lax.psum_scatter(partial_value, "heads", scatter_dimension=1, tiled=True)
    hidden_sum = residual.astype(F32) + attention
    full_width = residual.shape[1] * lax.axis_size("heads")
    square = lax.psum(jnp.sum(hidden_sum * hidden_sum, axis=1), "heads")
    inv_rms = lax.rsqrt(square / full_width + EPS)
    normed = (hidden_sum * inv_rms[:, None] * post_gain).astype(BF16)
    tok_rows, top_count = expert_ids.shape
    row_count = lax.axis_size("rows")
    exp_dev = expert_up.shape[0]
    experts_all = exp_dev * row_count
    capacity = max(2, (tok_rows * top_count + experts_all - 1) // experts_all + 1)
    half_width = normed.shape[1]
    flat_ids = expert_ids.reshape(-1)
    onehot = (flat_ids[:, None] == jnp.arange(experts_all, dtype=jnp.int32)[None, :]).astype(
        jnp.int32
    )
    earlier = jnp.cumsum(onehot, axis=0) - onehot
    slot_index = jnp.sum(earlier * onehot, axis=1)
    position = (flat_ids % exp_dev * row_count + flat_ids // exp_dev) * capacity + slot_index
    select = (
        jnp.arange(experts_all * capacity, dtype=jnp.int32)[:, None] == position[None, :]
    ).astype(BF16)
    spread = jnp.repeat(normed, top_count, axis=0)
    outgoing = jnp.dot(select, spread, preferred_element_type=F32).astype(BF16)
    outgoing = outgoing.reshape(exp_dev, row_count, capacity, half_width)
    arrived = lax.all_to_all(outgoing, "rows", split_axis=1, concat_axis=1, tiled=True)
    rows_in = arrived.reshape(exp_dev, row_count * capacity, half_width)
    partial_up = jnp.einsum("lnd,ldf->lnf", rows_in, expert_up, preferred_element_type=F32)
    full_up = lax.psum(partial_up, "heads")
    inner_width = expert_down.shape[1]
    activation = (jax.nn.silu(full_up[..., :inner_width]) * full_up[..., inner_width:]).astype(BF16)
    result = jnp.einsum("lnf,lfd->lnd", activation, expert_down, preferred_element_type=F32)
    returned = lax.all_to_all(
        result.astype(BF16).reshape(exp_dev, row_count, capacity, half_width),
        "rows",
        split_axis=1,
        concat_axis=1,
        tiled=True,
    )
    values_back = jnp.dot(select.T, returned.reshape(-1, half_width), preferred_element_type=F32)
    values_back = values_back.reshape(tok_rows, top_count, half_width)
    weights = expert_scores / jnp.sum(expert_scores, axis=1, keepdims=True)
    return (hidden_sum + jnp.sum(weights[:, :, None] * values_back, axis=1)).astype(BF16)


def per_device(mesh_shape, *args):
    delta_args, layer_args = args[:11], args[11:]
    rows = mesh_shape["rows"]
    if mesh_shape["heads"] == 1 and rows in (8, 16):
        line = rows // 4
        out_weight, residual, post_gain, ids, scores, up, down = layer_args
        *packed, kept_state = delta_rule(*delta_args, line, residual, ids, scores)
        layer_out = plane_layer(line, packed, out_weight, residual, post_gain, up, down)
    else:
        mixed, kept_state = delta_rule(*delta_args)
        layer_out = general_layer(mixed, *layer_args)
    return (layer_out, kept_state)


def solution(mesh):
    return jax.shard_map(
        functools.partial(per_device, dict(mesh.shape)),
        mesh=mesh,
        in_specs=(
            P(("groups", "rows"), "heads"),
            P(("groups", "rows"), "heads"),
            P(("groups", "rows"), "heads"),
            P(("groups", "rows"), "heads"),
            P(("groups", "rows"), "heads"),
            P(("groups", "rows"), "heads"),
            P("heads"),
            P("heads"),
            P(),
            P(("groups", "rows"), "heads", None, None),
            P(("groups", "rows")),
            P("heads", "rows"),
            P(("groups", "rows"), "heads"),
            P("heads"),
            P(("groups", "rows"), None),
            P(("groups", "rows"), None),
            P("rows", "heads", None),
            P("rows", None, "heads"),
        ),
        out_specs=(P(("groups", "rows"), "heads"), P(("groups", "rows"), "heads", None, None)),
        check_vma=False,
    )
```

```python
import functools

import jax
import jax.numpy as jnp
from jax import lax
from jax.experimental import pallas as pl
from jax.experimental.pallas import tpu as pltpu
from jax.sharding import PartitionSpec as P

EPS = 1e-06
BF16 = jnp.bfloat16
F32 = jnp.float32


def round_up(value, step):
    return -(-value // step) * step


def delta_kernel(
    drafts,
    group,
    line,
    accepted_ref,
    query_ref,
    key_ref,
    value_ref,
    gate_ref,
    decay_ref,
    beta_ref,
    rate_ref,
    bias_ref,
    gain_ref,
    state_ref,
    *refs,
):
    if line:
        residual_ref, ids_ref, scores_ref = refs[:3]
        packed_refs, refs = refs[3 : 3 + line], refs[3 + line :]
        written_ref, coef, unit, vals, mixed_ref, pack = refs
    else:
        mixed_ref, written_ref, coef, unit, vals = refs
    step = pl.program_id(0)
    tok = query_ref.shape[0]
    pad = unit.shape[1] // 2
    reqs, _, width, vwidth = state_ref.shape
    repeat = state_ref.shape[1] // group
    heads = decay_ref.shape[0]

    def shift(values, by):
        return pltpu.roll(values, by % pad, 0) if by % pad else values

    def ahead_of(values, by):
        return pltpu.roll(values, by % 128, 1) if by % 128 else values

    @pl.when(step == 0)
    def _():
        unit[...] = jnp.zeros_like(unit)
        vals[...] = jnp.zeros_like(vals)
        coef[...] = jnp.zeros_like(coef)
        square = (heads, heads)
        eye = lax.broadcasted_iota(jnp.int32, square, 0) == lax.broadcasted_iota(jnp.int32, square, 1)
        rate = jnp.sum(jnp.where(eye, rate_ref[...], 0.0), axis=1, keepdims=True)
        bias = jnp.sum(jnp.where(eye, bias_ref[...], 0.0), axis=1, keepdims=True)
        coef[0:heads, 0:tok] = -rate * jax.nn.softplus(decay_ref[...] + bias)
        coef[heads : 2 * heads, 0:tok] = jax.nn.sigmoid(beta_ref[...])
        log_decay = coef[0:heads]
        at = lax.broadcasted_iota(jnp.int32, log_decay.shape, 1)
        draft = at % drafts
        left = jnp.zeros_like(at)
        for r in range(reqs):
            left = jnp.where(at // drafts == r, accepted_ref[r], left)
        left = left - 1 - draft
        sums = [jnp.zeros_like(log_decay)]
        for o in range(drafts):
            sums.append(sums[-1] + ahead_of(log_decay, o))
        total = sums[1]
        for s in range(1, drafts):
            total = jnp.where(draft == s, sums[s + 1], total)
        coef[0:heads] = jnp.exp(total)
        for o in range(1, drafts):
            coef[(1 + o) * heads : (2 + o) * heads] = jnp.where(draft >= o, jnp.exp(sums[o]), 0.0)
        ahead = jnp.zeros_like(log_decay)
        later = jnp.zeros_like(log_decay)
        for o in range(1, drafts):
            ahead = ahead + ahead_of(log_decay, -o)
            later = jnp.where(left == o, ahead, later)
        coef[(1 + drafts) * heads : (2 + drafts) * heads] = jnp.where(
            left >= 0, jnp.exp(later), 0.0
        )
        coef[(2 + drafts) * heads : (3 + drafts) * heads] = jnp.exp(total + later)
        coef[...] = coef[...].T
        if line:
            rows = pack.shape[0] // 2
            half = mixed_ref.shape[1] // 2
            scores = scores_ref[...]
            scores = scores / jnp.sum(scores, axis=0, keepdims=True)
            experts = 64
            number = lax.broadcasted_iota(jnp.int32, (experts, tok), 0)
            dense = jnp.zeros((experts, tok), F32)
            for k in range(ids_ref.shape[0]):
                dense = dense + jnp.where(number == ids_ref[k : k + 1, :], scores[k : k + 1], 0.0)
            high = dense.astype(BF16).astype(F32)
            routes = jnp.concatenate([high, dense - high], axis=0)
            routes = jnp.concatenate(
                [routes, jnp.zeros((2 * experts, 128 - tok), F32)], axis=1
            ).T
            pack[...] = jnp.zeros_like(pack)
            part = mixed_ref.shape[1] // line
            at = half + part - (pack.shape[1] - half)
            pack[rows : 2 * rows, at : at + 128] = routes[0:tok]

    lane = lax.broadcasted_iota(jnp.int32, (pad, coef.shape[1]), 1)
    row = lax.broadcasted_iota(jnp.int32, (2 * pad, width), 0)
    request = row % pad // drafts
    for i in range(group):
        cols = slice(i * width, (i + 1) * width)
        for slot, ref, factor in ((0, query_ref, width ** (-0.5)), (1, key_ref, 1.0)):
            raw = ref[:, cols].astype(F32)
            scale = lax.rsqrt(jnp.sum(raw * raw, axis=1, keepdims=True) + EPS) * factor
            unit[i, slot * pad : slot * pad + tok, :] = raw * scale
        both = unit[i]
        high = both.astype(BF16).astype(F32)
        low = both - high
        spread = []
        for r in range(reqs):
            part = request == r
            spread.append(
                jnp.concatenate(
                    [jnp.where(part, high, 0.0), jnp.where(part, low, 0.0)], axis=0
                ).astype(BF16)
            )
        spread = jnp.concatenate(spread, axis=1)
        prior = jnp.concatenate(
            [
                jnp.concatenate([state_ref[r, repeat * i + j] for j in range(repeat)], axis=1)
                for r in range(reqs)
            ],
            axis=0,
        )
        read = jnp.dot(spread, prior, preferred_element_type=F32)
        query_prior = read[0:pad] + read[2 * pad : 3 * pad]
        key_prior = read[pad : 2 * pad] + read[3 * pad : 4 * pad]
        query, key = both[0:pad], both[pad : 2 * pad]
        shifted = [shift(key, o) for o in range(drafts)]
        query_key = [jnp.sum(query * s, axis=1, keepdims=True) for s in shifted]
        key_key = [jnp.sum(key * s, axis=1, keepdims=True) for s in shifted]
        for j in range(repeat):
            head = (step * group + i) * repeat + j
            vcols = slice((repeat * i + j) * vwidth, (repeat * i + j + 1) * vwidth)
            at = slice(j * vwidth, (j + 1) * vwidth)

            def column(index):
                mine = jnp.where(lane == index * heads + head, coef[0:pad], 0.0)
                return jnp.sum(mine, axis=1, keepdims=True)

            through, rate = column(0), column(1)
            decays = [column(1 + o) for o in range(1, drafts)]
            vals[j, 0:tok, :] = value_ref[:, vcols].astype(F32)
            base = rate * (vals[j] - through * key_prior[:, at])
            mixes = [rate * decays[o - 1] * key_key[o] for o in range(1, drafts)]
            delta = base
            for _ in range(1, drafts):
                delta = base - sum(mixes[o - 1] * shift(delta, o) for o in range(1, drafts))
            out = through * query_prior[:, at] + query_key[0] * delta
            for o in range(1, drafts):
                out = out + (decays[o - 1] * query_key[o]) * shift(delta, o)
            norm = lax.rsqrt(jnp.mean(out * out, axis=1, keepdims=True) + EPS)
            gate = gate_ref[:, vcols].astype(F32)
            mixed = (out * norm)[0:tok] * gain_ref[...] * jax.nn.silu(gate)
            if line:
                span = group * repeat * vwidth
                to = pl.multiple_of(step * span, span) + (repeat * i + j) * vwidth
                mixed_ref[0:tok, pl.ds(to, vwidth)] = mixed
            else:
                mixed_ref[:, vcols] = mixed.astype(BF16)
            written_ref[:, vcols] = column(1 + drafts) * delta
    if not line:
        return

    @pl.when(step == pl.num_programs(0) - 1)
    def _():
        here = lax.axis_index("rows") // 4
        full = mixed_ref.shape[1]
        half, part = full // 2, full // line
        extra = pack.shape[1] - half
        pack[0:tok, 0:half] = mixed_ref[0:tok, 0:half]
        pack[tok : 2 * tok, 0:half] = mixed_ref[0:tok, half:full]
        for m in range(line):
            to = pl.multiple_of((here ^ m) * part, part)
            piece = residual_ref[:, pl.ds(to, part)].astype(F32)
            pack[0:tok, half : half + extra] = piece[:, 0:extra]
            pack[tok : 2 * tok, half : half + part - extra] = piece[:, extra:part]
            packed_refs[m][...] = pack[...].astype(BF16)


def kept_kernel(
    drafts, group, key_ref, written_ref, coef_ref, state_ref, kept_ref, unit
):
    step = pl.program_id(0)
    tok = key_ref.shape[0]
    pad = written_ref.shape[0]
    reqs, _, width, vwidth = state_ref.shape
    repeat = state_ref.shape[1] // group
    heads = pl.num_programs(0) * group * repeat

    @pl.when(step == 0)
    def _():
        unit[...] = jnp.zeros_like(unit)

    lane = lax.broadcasted_iota(jnp.int32, (pad, coef_ref.shape[1]), 1)
    request = lax.broadcasted_iota(jnp.int32, (3 * pad, width), 0) % pad // drafts
    for i in range(group):
        raw = key_ref[:, i * width : (i + 1) * width].astype(F32)
        unit[i, 0:tok, :] = raw * lax.rsqrt(jnp.sum(raw * raw, axis=1, keepdims=True) + EPS)
        key = unit[i]
        high = key.astype(BF16).astype(F32)
        key = jnp.concatenate([high, high, key - high], axis=0)
        spread = jnp.concatenate(
            [jnp.where(request == r, key, 0.0).astype(BF16) for r in range(reqs)], axis=1
        )
        written = written_ref[:, i * repeat * vwidth : (i + 1) * repeat * vwidth]
        high = written.astype(BF16).astype(F32)
        wrote = jnp.concatenate([high, written - high, high], axis=0).astype(BF16)
        update = lax.dot_general(
            spread, wrote, (((0,), (0,)), ((), ())), preferred_element_type=F32
        )
        for j in range(repeat):
            head = (step * group + i) * repeat + j
            mine = jnp.where(lane == (2 + drafts) * heads + head, coef_ref[0:pad], 0.0)
            keep = jnp.broadcast_to(jnp.sum(mine, axis=1, keepdims=True), (pad, vwidth))
            for r in range(reqs):
                kept_ref[r, repeat * i + j] = (
                    keep[r * drafts : r * drafts + 1, :] * state_ref[r, repeat * i + j].astype(F32)
                    + update[r * width : (r + 1) * width, j * vwidth : (j + 1) * vwidth]
                ).astype(BF16)


def delta_rule(
    query_in,
    key_in,
    value_in,
    gate_in,
    decay_in,
    beta_in,
    decay_rate,
    decay_bias,
    norm_gain,
    prior_state,
    accepted,
    line=0,
    residual=None,
    expert_ids=None,
    expert_scores=None,
):
    tok = query_in.shape[0]
    reqs, heads, width, vwidth = prior_state.shape
    drafts = tok // reqs
    query_heads = query_in.shape[1] // width
    repeat = heads // query_heads
    group = 4 if query_heads % 4 == 0 else 1
    pad = round_up(tok, 8)
    whole = lambda *shape: pl.BlockSpec(shape, lambda g: (0,) * len(shape))
    qblock = pl.BlockSpec((tok, group * width), lambda g: (0, g))
    vblock = pl.BlockSpec((tok, group * repeat * vwidth), lambda g: (0, g))
    sblock = pl.BlockSpec((reqs, group * repeat, width, vwidth), lambda g: (0, g, 0, 0))
    in_specs = [
        pl.BlockSpec(memory_space=pltpu.SMEM),
        qblock,
        qblock,
        vblock,
        vblock,
        whole(heads, tok),
        whole(heads, tok),
        whole(1, heads),
        whole(1, heads),
        whole(1, vwidth),
        sblock,
    ]
    args = [
        accepted,
        query_in,
        key_in,
        value_in,
        gate_in,
        decay_in.T,
        beta_in.T,
        decay_rate.reshape(1, heads),
        decay_bias.reshape(1, heads),
        norm_gain.reshape(1, vwidth),
        prior_state,
    ]
    scratch = [
        pltpu.VMEM((group, 2 * pad, width), F32),
        pltpu.VMEM((repeat, pad, vwidth), F32),
    ]
    full = heads * vwidth
    out_specs = [pl.BlockSpec((pad, group * repeat * vwidth), lambda g: (0, g)), whole(128, 128)]
    out_shape = [jax.ShapeDtypeStruct((pad, full), F32), jax.ShapeDtypeStruct((128, 128), F32)]
    if line:
        packed = packed_shape(tok, full, line)
        out_specs = [whole(*packed)] * line + out_specs
        out_shape = [jax.ShapeDtypeStruct(packed, BF16)] * line + out_shape
        scratch += [pltpu.VMEM((pad, full), F32), pltpu.VMEM(packed, F32)]
        top = expert_ids.shape[1]
        in_specs += [whole(tok, full), whole(top, tok), whole(top, tok)]
        args += [residual, expert_ids.T, expert_scores.T]
    else:
        out_specs = [vblock] + out_specs
        out_shape = [jax.ShapeDtypeStruct((tok, full), BF16)] + out_shape
    cells = heads * reqs * width * vwidth
    grid = (query_heads // group,)
    *mixed, written, coef = pl.pallas_call(
        functools.partial(delta_kernel, drafts, group, line),
        grid=grid,
        in_specs=in_specs,
        out_specs=out_specs,
        out_shape=out_shape,
        scratch_shapes=scratch,
        compiler_params=pltpu.CompilerParams(vmem_limit_bytes=56 * 1024 * 1024),
        cost_estimate=pl.CostEstimate(
            flops=512 * cells, bytes_accessed=4 * cells, transcendentals=0
        ),
    )(*args)
    kept = pl.pallas_call(
        functools.partial(kept_kernel, drafts, group),
        grid=grid,
        in_specs=[
            qblock,
            pl.BlockSpec((pad, group * repeat * vwidth), lambda g: (0, g)),
            whole(128, 128),
            sblock,
        ],
        out_specs=sblock,
        out_shape=jax.ShapeDtypeStruct(prior_state.shape, BF16),
        scratch_shapes=[pltpu.VMEM((group, pad, width), F32)],
        compiler_params=pltpu.CompilerParams(vmem_limit_bytes=56 * 1024 * 1024),
        cost_estimate=pl.CostEstimate(
            flops=512 * cells, bytes_accessed=4 * cells, transcendentals=0
        ),
    )(key_in, written, coef, prior_state)
    return (*mixed, kept)


def packed_shape(tok, full, line):
    return (2 * tok, full // 2 + round_up(full // line + 128, 256) // 2)


def swap(values, mask):
    count = lax.axis_size("rows")
    return lax.ppermute(values, "rows", [(i, i ^ mask) for i in range(count)])


def run_experts(tokens, routes, pairs):
    total = None
    half = routes.shape[1] // 2
    for up, down, first in pairs:
        inner = down.shape[1]
        wide = jnp.broadcast_to(tokens, (up.shape[0], *tokens.shape))
        full = jnp.einsum("lnd,ldf->lnf", wide, up, preferred_element_type=F32)
        acts = []
        for i in range(up.shape[0]):
            here = lax.dynamic_slice(routes, (0, first + i), (routes.shape[0], 1)).astype(F32)
            rest = lax.dynamic_slice(routes, (0, half + first + i), (routes.shape[0], 1))
            act = jax.nn.silu(full[i][:, :inner]) * full[i][:, inner:]
            acts.append((act * (here + rest.astype(F32))).astype(BF16))
        term = jnp.dot(
            jnp.concatenate(acts, axis=1),
            down.reshape(-1, down.shape[2]),
            preferred_element_type=F32,
        )
        total = term if total is None else total + term
    return total


def plane_layer(
    line,
    packed,
    out_weight,
    residual,
    post_gain,
    expert_up,
    expert_down,
):
    me = lax.axis_index("rows")
    here = me // 4
    tok, full = residual.shape
    exp_dev = expert_up.shape[0]
    part, half = full // line, full // 2
    extra = packed[0].shape[1] - half
    others = range(1, line)

    weight_x = swap(out_weight, 2)
    weight_core = swap(out_weight, 1)

    got = [packed[0]] + [swap(packed[m], 4 * m) for m in others]
    got[line // 2], weight_x = lax.optimization_barrier((got[line // 2], weight_x))
    weights = [out_weight, weight_core, weight_x, swap(weight_x, 1)]
    expert_up, expert_down, weights[3] = lax.optimization_barrier(
        (expert_up, expert_down, weights[3])
    )
    up_mate = swap(expert_up, 1)
    down_mate = swap(expert_down, 1)
    heads_in = [jnp.concatenate([g[:tok, :half], g[tok:, :half]], axis=1) for g in got]
    heads_in = jnp.concatenate(heads_in, axis=0)
    base = [
        jnp.concatenate([g[:tok, half:], g[tok:, half : half + part - extra]], axis=1) for g in got
    ]
    at = half + part - extra
    routes = jnp.concatenate([g[tok:, at : at + 128] for g in got], axis=0)
    attention = jnp.zeros((line * tok, part), F32)
    for mask, weight in enumerate(weights):
        piece = jnp.dot(heads_in, weight, preferred_element_type=F32)
        attention = lax.dynamic_update_slice(
            attention, piece, (0, ((me % 4) ^ mask) * piece.shape[1])
        )
    owner = jnp.arange(line * tok)[:, None] // tok
    base = jnp.concatenate(base, axis=0).astype(F32)
    columns = [(attention + jnp.where(owner == m, 0.0, base)).astype(BF16) for m in range(line)]

    hidden = jnp.zeros((line * tok, full), BF16)
    for m in range(line):
        piece = columns[m] if m == 0 else swap(columns[m], 4 * m)
        order = [piece[tok * (j ^ m) : tok * (j ^ m) + tok] for j in range(line)]
        hidden = lax.dynamic_update_slice(
            hidden, jnp.concatenate(order, axis=0), (0, (here ^ m) * part)
        )
    hidden = hidden.astype(F32)
    mine = hidden[:tok] + residual.astype(F32)
    hidden = jnp.concatenate([mine, hidden[tok:]], axis=0)
    scale = lax.rsqrt(jnp.mean(hidden * hidden, axis=1, keepdims=True) + EPS)
    normed = (hidden * scale * post_gain).astype(BF16)

    came = swap(normed, 2)
    far_routes = swap(routes, 2)
    pairs = [(expert_up, expert_down, me * exp_dev), (up_mate, down_mate, (me ^ 1) * exp_dev)]
    own_sum = run_experts(normed, routes, pairs)
    far_sum = run_experts(came, far_routes, pairs)
    total = own_sum + swap(far_sum.astype(BF16), 2).astype(F32)
    folded = []
    for m in range(line):
        rows = total[m * tok : (m + 1) * tok]
        folded.append(jnp.concatenate([rows[:, :half], rows[:, half:]], axis=0))
    out = folded[0]
    for m in others:
        out = out + swap(folded[m].astype(BF16), 4 * m).astype(F32)
    out = mine + jnp.concatenate([out[:tok], out[tok:]], axis=1)
    return out.astype(BF16)


def general_layer(
    mixed,
    out_weight,
    residual,
    post_gain,
    expert_ids,
    expert_scores,
    expert_up,
    expert_down,
):
    partial_value = jnp.dot(
        mixed,
        lax.all_gather(out_weight, "rows", axis=1, tiled=True),
        preferred_element_type=F32,
    )
    attention = lax.psum_scatter(partial_value, "heads", scatter_dimension=1, tiled=True)
    hidden_sum = residual.astype(F32) + attention
    full_width = residual.shape[1] * lax.axis_size("heads")
    square = lax.psum(jnp.sum(hidden_sum * hidden_sum, axis=1), "heads")
    inv_rms = lax.rsqrt(square / full_width + EPS)
    normed = (hidden_sum * inv_rms[:, None] * post_gain).astype(BF16)
    tok_rows, top_count = expert_ids.shape
    row_count = lax.axis_size("rows")
    exp_dev = expert_up.shape[0]
    experts_all = exp_dev * row_count
    capacity = max(2, (tok_rows * top_count + experts_all - 1) // experts_all + 1)
    half_width = normed.shape[1]
    flat_ids = expert_ids.reshape(-1)
    onehot = (flat_ids[:, None] == jnp.arange(experts_all, dtype=jnp.int32)[None, :]).astype(
        jnp.int32
    )
    earlier = jnp.cumsum(onehot, axis=0) - onehot
    slot_index = jnp.sum(earlier * onehot, axis=1)
    position = (flat_ids % exp_dev * row_count + flat_ids // exp_dev) * capacity + slot_index
    select = (
        jnp.arange(experts_all * capacity, dtype=jnp.int32)[:, None] == position[None, :]
    ).astype(BF16)
    spread = jnp.repeat(normed, top_count, axis=0)
    outgoing = jnp.dot(select, spread, preferred_element_type=F32).astype(BF16)
    outgoing = outgoing.reshape(exp_dev, row_count, capacity, half_width)
    arrived = lax.all_to_all(outgoing, "rows", split_axis=1, concat_axis=1, tiled=True)
    rows_in = arrived.reshape(exp_dev, row_count * capacity, half_width)
    partial_up = jnp.einsum("lnd,ldf->lnf", rows_in, expert_up, preferred_element_type=F32)
    full_up = lax.psum(partial_up, "heads")
    inner_width = expert_down.shape[1]
    activation = (jax.nn.silu(full_up[..., :inner_width]) * full_up[..., inner_width:]).astype(BF16)
    result = jnp.einsum("lnf,lfd->lnd", activation, expert_down, preferred_element_type=F32)
    returned = lax.all_to_all(
        result.astype(BF16).reshape(exp_dev, row_count, capacity, half_width),
        "rows",
        split_axis=1,
        concat_axis=1,
        tiled=True,
    )
    values_back = jnp.dot(select.T, returned.reshape(-1, half_width), preferred_element_type=F32)
    values_back = values_back.reshape(tok_rows, top_count, half_width)
    weights = expert_scores / jnp.sum(expert_scores, axis=1, keepdims=True)
    return (hidden_sum + jnp.sum(weights[:, :, None] * values_back, axis=1)).astype(BF16)


def per_device(mesh_shape, *args):
    delta_args, layer_args = args[:11], args[11:]
    rows = mesh_shape["rows"]
    if mesh_shape["heads"] == 1 and rows in (8, 16):
        line = rows // 4
        out_weight, residual, post_gain, ids, scores, up, down = layer_args
        *packed, kept_state = delta_rule(*delta_args, line, residual, ids, scores)
        layer_out = plane_layer(line, packed, out_weight, residual, post_gain, up, down)
    else:
        mixed, kept_state = delta_rule(*delta_args)
        layer_out = general_layer(mixed, *layer_args)
    return (layer_out, kept_state)


def solution(mesh):
    return jax.shard_map(
        functools.partial(per_device, dict(mesh.shape)),
        mesh=mesh,
        in_specs=(
            P(("groups", "rows"), "heads"),
            P(("groups", "rows"), "heads"),
            P(("groups", "rows"), "heads"),
            P(("groups", "rows"), "heads"),
            P(("groups", "rows"), "heads"),
            P(("groups", "rows"), "heads"),
            P("heads"),
            P("heads"),
            P(),
            P(("groups", "rows"), "heads", None, None),
            P(("groups", "rows")),
            P("heads", "rows"),
            P(("groups", "rows"), "heads"),
            P("heads"),
            P(("groups", "rows"), None),
            P(("groups", "rows"), None),
            P("rows", "heads", None),
            P("rows", None, "heads"),
        ),
        out_specs=(P(("groups", "rows"), "heads"), P(("groups", "rows"), "heads", None, None)),
        check_vma=False,
    )
```
